128 devices in a mesh: region: 32 (over y, x, core), band: 4 (over z).
Axes of the slice: x: 4, y: 4, z: 4, core: 2. Of those that a mesh axis runs over, the one named last changes fastest.
Arguments:
- anomalies: bfloat16 [2097152, 128], P(('region', 'band')), may hold values from -28 to 28
- operator: bfloat16 [2048, 4, 128, 128], P(('region', 'band')), may hold values from -0.0014648438 to 0.0014648438
- local_tile_index: int32 [2048, 4], P(('region', 'band')), may hold values from 0 to 127
- err_std: float32 [262144], P(('region', 'band')), may hold values from 3 to 58
- err_corr: float32 [262144], P(('region', 'band')), may hold values from -1 to 1
Outputs:
- whitened: float32 [262144, 128], P(('region', 'band'))
- updated: bfloat16 [2097152, 128], P(('region', 'band'))
The draws below stay inside these ranges and needn't reach their ends.
Inputs may be any that keep to these rules, and one draw needn't show every extreme that they name: `local_tile_index`: entry [j, k] names a tile of the device that lies k places further along band, cyclically, in the region of the device that holds block j.
All inputs are finite; a program needn't handle non-finite values.
Results may differ from the reference program's by a relative error of at most 0.0043.
The reference program's roundings to bfloat16 on the way (of `transform`) count: a program that leaves them out, or rounds other values in their place, can miss the bound.
Values may be sent and summed in bfloat16 or wider, within the bound.
A program may use at most 64 MiB of HBM per device.

```python
import math
import jax
import jax.numpy as jnp
from jax import lax

M = 128
TILE = 128
TILES_DEV = 128
BLK_DEV = 16
NODES = 2097152
OBS_BLOCKS = 2048
NOBS = 262144
N_BAND = 4


def draw_anomalies(key, part):
    keys = jax.random.split(jax.random.fold_in(key, 11), 4)
    noise = jnp.clip(jax.random.normal(keys[0], (NODES, M), jnp.float32), -4.0, 4.0)
    common_weight = 0.5
    member_scale = jnp.exp(jax.random.uniform(keys[1], (1, M), jnp.float32, math.log(0.5), math.log(2.0)))
    node_factors = jnp.clip(jax.random.normal(keys[2], (NODES, 3), jnp.float32), -3.0, 3.0)
    member_factors = jnp.clip(jax.random.normal(keys[3], (3, M), jnp.float32), -3.0, 3.0)
    common = node_factors[:, 0:1] * member_factors[0:1, :]
    common = common + node_factors[:, 1:2] * member_factors[1:2, :]
    common = common + node_factors[:, 2:3] * member_factors[2:3, :]
    return (noise * member_scale + common_weight * common).astype(jnp.bfloat16)


def draw_err_std(key, part):
    keys = jax.random.split(jax.random.fold_in(key, 23), 1)
    position = jnp.arange(NOBS, dtype=jnp.float32) / max(NOBS - 1, 1)
    base = jnp.exp(jax.random.uniform(keys[0], (NOBS,), jnp.float32, math.log(3.0), math.log(18.0)))
    trend = jnp.exp((1.0 - position) * math.log(1.8))
    return (base * trend).astype(jnp.float32)


def draw_err_corr(key, part):
    keys = jax.random.split(jax.random.fold_in(key, 37), 4)
    levels = NOBS // TILE
    level_rate = jnp.exp(jax.random.uniform(keys[0], (levels,), jnp.float32, math.log(0.5), math.log(2.0)))
    keep_low = 0.62
    rate = jnp.repeat(level_rate, TILE)
    absolute_size = 1.0 - rate * (0.7 / NOBS)
    spots = jax.random.randint(keys[1], (3,), 0, NOBS)
    retained_flags = jax.random.uniform(keys[2], (3,), jnp.float32, keep_low, 0.8)
    position = jnp.arange(NOBS, dtype=jnp.int32)
    match_found = position[:, None] == spots[None, :]
    sudden_jump = jnp.prod(jnp.where(match_found, retained_flags[None, :], 1.0), axis=1)
    sign_pattern = jnp.where(jax.random.bernoulli(keys[3], 0.5, (NOBS,)), 1.0, -1.0)
    return (sign_pattern * absolute_size * sudden_jump).astype(jnp.float32)


def plant(result, stream_key, smallest, top_value):
    place = [jax.random.randint(jax.random.fold_in(stream_key, axis), (), 0, length) for axis, length in enumerate(result.shape)]
    longest = result.shape.index(max(result.shape))
    neighbour = place[:longest] + [(place[longest] + 1) % result.shape[longest]] + place[longest + 1:]
    return result.at[tuple(place)].set(smallest).at[tuple(neighbour)].set(top_value)


def steps_of(own_key, extent, cuts, smallest, top_value):
    def one(dim, shards_of):
        steps = jax.random.uniform(jax.random.fold_in(jax.random.fold_in(own_key, 6), dim), (shards_of,), jnp.float32, smallest / len(cuts), top_value / len(cuts))
        return jnp.repeat(jnp.exp(steps), extent[dim] // shards_of).reshape((-1,) + (1,) * (len(extent) - dim - 1))

    gain = one(*cuts[0])
    for cut in cuts[1:]:
        gain = gain * one(*cut)
    return gain


def gaussian(rng, shape, width, reach, shards=(), kind=jnp.bfloat16):
    result = jax.random.normal(rng, shape, jnp.float32) * width
    if len(shards) > 0:
        result = steps_of(rng, shape, shards, -0.22, 0.18) * result
    return jnp.clip(result, min=-reach, max=reach).astype(kind)


def setup_inputs(seed: int = 0) -> dict:
    seeds = jax.random.split(jax.random.key(seed), 6)
    anomalies = draw_anomalies(jax.random.fold_in(seeds[5], 71), 0)
    operator = gaussian(seeds[1], (OBS_BLOCKS, N_BAND, TILE, TILE), (N_BAND * TILE * NOBS // 8) ** -0.5, 0.0014648438, ((0, 128),))
    local_tile_index = plant(jax.random.randint(seeds[2], (OBS_BLOCKS, N_BAND), 0, TILES_DEV), jax.random.fold_in(seeds[2], 1), 0, TILES_DEV - 1).astype(jnp.int32)
    err_std = draw_err_std(jax.random.fold_in(seeds[5], 71), 0)
    err_corr = draw_err_corr(jax.random.fold_in(seeds[5], 71), 0)
    return dict(anomalies=anomalies, operator=operator, local_tile_index=local_tile_index, err_std=err_std, err_corr=err_corr)


def affine_link(earlier, trailing):
    return (earlier[0] * trailing[0], trailing[0] * earlier[1] + trailing[1])

def reference(anomalies, operator, local_tile_index, err_std, err_corr):
    members = anomalies.shape[1]
    groups = OBS_BLOCKS // BLK_DEV
    tiles_all = anomalies.reshape(-1, TILE, members)
    block_ids = jnp.arange(OBS_BLOCKS, dtype=jnp.int32)
    holder = block_ids // BLK_DEV
    region_of = holder // N_BAND
    band_of = holder % N_BAND
    offsets = jnp.arange(N_BAND, dtype=jnp.int32)
    target = region_of[:, None] * N_BAND + (band_of[:, None] + offsets[None, :]) % N_BAND
    node_tile = (target * TILES_DEV + local_tile_index.astype(jnp.int32)).astype(jnp.int32)

    def single_cluster(group_pair):
        op_blocks, tile_picks = group_pair
        picked = jnp.take(tiles_all, tile_picks, axis=0).astype(jnp.float32)
        return jnp.einsum('jkon,jknm->jom', op_blocks.astype(jnp.float32), picked, precision=lax.Precision.HIGHEST)
    predicted = lax.map(single_cluster, (operator.reshape(groups, BLK_DEV, N_BAND, TILE, TILE), node_tile.reshape(groups, BLK_DEV, N_BAND)))
    predicted = predicted.reshape(-1, members)
    rescaled_values = predicted / err_std[:, None]
    decay_coef = err_corr[:, None]
    _, whitened = lax.associative_scan(affine_link, (decay_coef, rescaled_values), axis=0)
    gram_total = (members - 1.0) * jnp.eye(members, dtype=jnp.float32) + jnp.dot(whitened.T.astype(jnp.float32), whitened.astype(jnp.float32), precision=lax.Precision.HIGHEST, preferred_element_type=jnp.float32)
    lower_factor = jnp.linalg.cholesky(gram_total)
    inverse = lax.linalg.triangular_solve(lower_factor, jnp.eye(members, dtype=jnp.float32), left_side=True, lower=True, transpose_a=True)
    transform = (math.sqrt(members - 1.0) * inverse).astype(jnp.bfloat16)

    def update(row_block):
        return jnp.dot(row_block.astype(jnp.float32), transform.astype(jnp.float32), preferred_element_type=jnp.float32).astype(jnp.bfloat16)
    updated = lax.map(update, anomalies.reshape(groups, -1, members)).reshape(-1, members)
    return (whitened, updated)
```

```python
import functools
import math

import jax
import jax.numpy as jnp
from jax import lax
from jax.experimental import pallas as pl
from jax.experimental.pallas import tpu as pltpu
from jax.sharding import PartitionSpec as P

MESH = pl.DeviceIdType.MESH
HIGHEST = lax.Precision.HIGHEST
F32 = jnp.float32
BF16 = jnp.bfloat16

M = 128
BLK = 16
BAND = 4
CHUNK = 2
CHUNKS = BLK // CHUNK
NEAR = 8
FAR = 16
ROWS = M // NEAR


def block_scan(decay, value):
    row = lax.broadcasted_iota(jnp.int32, (M, M), 0)
    for d in (1, 2, 4):
        seen = row >= d
        before_v = jnp.where(seen, pltpu.roll(value, d, 0), 0.0)
        before_d = jnp.where(seen, pltpu.roll(decay, d, 0), 1.0)
        value = value + decay * before_v
        decay = decay * before_d
    for d in (8, 16, 32, 64):
        value = jnp.concatenate([value[:d], value[d:] + decay[d:] * value[:-d]], axis=0)
        decay = jnp.concatenate([decay[:d], decay[d:] * decay[:-d]], axis=0)
    return decay, value


def as_columns(row):
    return jnp.broadcast_to(row, (M, M)).T


def combine(n, me, rows_at, parts, left, right, whole):
    carry = jnp.zeros((1, M), F32)
    product = jnp.ones((1, M), F32)
    cross = jnp.zeros((1, M), F32)
    square = jnp.zeros((1, M), F32)
    own_carry, own_product = carry, product
    rows = jnp.zeros((ROWS, M), F32)
    for i in range(n):
        rows = rows + parts[i, 0:ROWS]
        state = parts[i, ROWS : ROWS + 8]
        a, b, h, s = (state[k : k + 1] for k in range(4))
        mine = me == i
        own_carry = jnp.where(mine, carry, own_carry)
        own_product = jnp.where(mine, product, own_product)
        u = h + s * carry
        left[i : i + 1, :] = h
        left[n + i : n + i + 1, :] = carry
        right[i : i + 1, :] = carry
        right[n + i : n + i + 1, :] = u
        cross = cross + product * u
        square = square + product * product * s
        carry = b + a * carry
        product = product * a
    whole[...] = jnp.dot(left[...].T, right[...], precision=HIGHEST, preferred_element_type=F32)
    rows = rows + whole[pl.ds(pl.multiple_of(rows_at, ROWS), ROWS), :]
    state = jnp.concatenate([product, carry, cross, square, jnp.zeros((4, M), F32)], axis=0)
    return rows, state, own_carry, own_product


def observe(
    anom_hbm, op_hbm, idx_vm, std_vm, corr_vm,
    gram_out, whit_out,
    anom, op, idx_own, idx_in, idx, send, recv, whit, prod, gram, msg1, in1, msg2, in2, l1, r1, l2, r2, whole, gram_in,
    load_sem, idx_sem, idx_send, idx_recv, tile_send, tile_recv, s1, q1, s2, q2, s3, q3,
):
    region, band = lax.axis_index("region"), lax.axis_index("band")
    column, core = region // 2, region % 2
    near = core * BAND + band

    load_anom = pltpu.make_async_copy(anom_hbm, anom, load_sem.at[0])
    load_op = pltpu.make_async_copy(op_hbm, op, load_sem.at[1])
    load_anom.start()
    load_op.start()

    def near_peer(e):
        p = (near + e) % NEAR
        return (column * 2 + p // BAND, p % BAND), p

    def far_peer(e):
        q = (column + e) % FAR
        return (q * 2 + core, band), q

    barrier = pltpu.get_barrier_semaphore()
    for e in range(1, NEAR):
        pl.semaphore_signal(barrier, inc=1, device_id=near_peer(e)[0], device_id_type=MESH)
    for e in range(1, FAR):
        pl.semaphore_signal(barrier, inc=1, device_id=far_peer(e)[0], device_id_type=MESH)

    idx_own[...] = jnp.zeros((8, M), jnp.int32)
    idx_own[0:BAND, 0:BLK] = idx_vm[...]
    own_idx = pltpu.make_async_copy(idx_own, idx.at[0], idx_sem.at[0])
    own_idx.start()
    pl.semaphore_wait(barrier, NEAR + FAR - 2)

    def idx_copy(e):
        return pltpu.make_async_remote_copy(
            src_ref=idx_own, dst_ref=idx_in.at[BAND - e], send_sem=idx_send.at[e], recv_sem=idx_recv.at[e],
            device_id=(region, (band + e) % BAND), device_id_type=MESH,
        )

    for e in (2, 1, 3):
        idx_copy(e).start()
    load_anom.wait()
    to_scalar = {}
    for e in (2, 1, 3):
        idx_copy(e).wait_recv()
        d = BAND - e
        to_scalar[d] = pltpu.make_async_copy(idx_in.at[d], idx.at[d], idx_sem.at[d])
        to_scalar[d].start()
    own_idx.wait()
    for e in (2, 1, 3):
        to_scalar[BAND - e].wait()

    def tile_copy(k, c):
        part = pl.ds(c * CHUNK, CHUNK)
        return pltpu.make_async_remote_copy(
            src_ref=send.at[k - 1, part], dst_ref=recv.at[k - 1, part],
            send_sem=tile_send.at[k - 1, c], recv_sem=tile_recv.at[k - 1, c],
            device_id=(region, (band + BAND - k) % BAND), device_id_type=MESH,
        )

    def serve(c, carry):
        for k in (2, 1, 3):
            for t in range(CHUNK):
                j = c * CHUNK + t
                send[k - 1, j] = anom[idx[BAND - k, k, j]]
            tile_copy(k, c).start()
        return carry

    lax.fori_loop(0, CHUNKS, serve, 0)
    load_op.wait()
    gram[...] = jnp.zeros((M, M), F32)

    def use(c, carry):
        last, product, cross, square = carry
        for k in (1, 3, 2):
            tile_copy(k, c).wait_recv()
        for t in range(CHUNK):
            j = c * CHUNK + t
            value = jnp.dot(op[j, 0], anom[idx[0, 0, j]], preferred_element_type=F32)
            for k in range(1, BAND):
                value = value + jnp.dot(op[j, k], recv[k - 1, j], preferred_element_type=F32)
            value = value * as_columns(1.0 / std_vm[pl.ds(j, 1), :])
            decay, value = block_scan(as_columns(corr_vm[pl.ds(j, 1), :]), value)
            value = value + decay * last
            decay = decay * product
            whit[j] = value
            prod[j] = decay
            last, product = value[M - 1 : M], decay[M - 1 : M]
            gram[...] += jnp.dot(value.T, value, precision=HIGHEST, preferred_element_type=F32)
            cross = cross + jnp.sum(value * decay, axis=0, keepdims=True)
            square = square + jnp.sum(decay * decay, axis=0, keepdims=True)
        return last, product, cross, square

    zero = jnp.zeros((1, M), F32)
    last, product, cross, square = lax.fori_loop(0, CHUNKS, use, (zero, jnp.ones((1, M), F32), zero, zero))

    state = jnp.concatenate([product, last, cross, square, jnp.zeros((4, M), F32)], axis=0)
    for p in range(NEAR):
        msg1[p, 0:ROWS] = gram[p * ROWS : (p + 1) * ROWS]
        msg1[p, ROWS : ROWS + 8] = state

    def copy1(e):
        device, p = near_peer(e)
        return pltpu.make_async_remote_copy(
            src_ref=msg1.at[p], dst_ref=in1.at[near], send_sem=s1.at[e], recv_sem=q1.at[e],
            device_id=device, device_id_type=MESH,
        )

    for e in range(1, NEAR):
        copy1(e).start()
    in1[near] = msg1[near]
    for e in range(1, NEAR):
        copy1(e).wait_recv()
    rows, state, own_carry, own_product = combine(NEAR, near, near * ROWS, in1, l1, r1, whole)
    msg2[0:ROWS] = rows
    msg2[ROWS : ROWS + 8] = state

    def copy2(e):
        device, _ = far_peer(e)
        return pltpu.make_async_remote_copy(
            src_ref=msg2, dst_ref=in2.at[column], send_sem=s2.at[e], recv_sem=q2.at[e],
            device_id=device, device_id_type=MESH,
        )

    for e in range(1, FAR):
        copy2(e).start()
    in2[column] = msg2[...]
    for e in range(1, FAR):
        copy2(e).wait_recv()
    rows, state, far_carry, _ = combine(FAR, column, near * ROWS, in2, l2, r2, whole)
    here = lax.broadcasted_iota(jnp.int32, (ROWS, M), 0) + near * ROWS
    lane = lax.broadcasted_iota(jnp.int32, (ROWS, M), 1)
    rows = rows + jnp.where(here == lane, M - 1.0, 0.0)
    own_rows = pl.ds(pl.multiple_of(near * ROWS, ROWS), ROWS)
    gram_in[own_rows, :] = rows

    def copy3(e):
        device, _ = near_peer(e)
        return pltpu.make_async_remote_copy(
            src_ref=gram_in.at[own_rows], dst_ref=gram_in.at[own_rows], send_sem=s3.at[e], recv_sem=q3.at[e],
            device_id=device, device_id_type=MESH,
        )

    for e in range(1, NEAR):
        copy3(e).start()

    before = own_carry + own_product * far_carry

    def settle(j, carry):
        whit[j] = whit[j] + prod[j] * before
        return carry

    lax.fori_loop(0, BLK, settle, 0)
    store = pltpu.make_async_copy(whit, whit_out, load_sem.at[0])
    store.start()
    for e in range(1, NEAR):
        copy3(e).wait_recv()
    gram_out[...] = gram_in[...]

    store.wait()
    for e in (2, 1, 3):
        idx_copy(e).wait_send()

    def drain(c, carry):
        for k in range(1, BAND):
            tile_copy(k, c).wait_send()
        return carry

    lax.fori_loop(0, CHUNKS, drain, 0)
    for e in range(1, NEAR):
        copy1(e).wait_send()
        copy3(e).wait_send()
    for e in range(1, FAR):
        copy2(e).wait_send()


def inverse_factor(work, gram):
    n = M // 8
    lane = lax.broadcasted_iota(jnp.int32, (8, M), 1)
    sub = lax.broadcasted_iota(jnp.int32, (8, M), 0)
    rows = [gram[8 * i : 8 * i + 8, :] for i in range(n)]
    done = []
    for p in range(n):
        base = 8 * p
        block = rows[p]
        cols = [jnp.broadcast_to(block[:, base + l : base + l + 1], (8, M)) for l in range(8)]
        s = [[jnp.broadcast_to(cols[l][j : j + 1, :], (8, M)) for l in range(8)] for j in range(8)]
        inside = (lane >= base) & (lane < base + 8)
        r = []
        for j in range(8):
            own = jnp.broadcast_to(block[j : j + 1, :], (8, M))
            r.append(jnp.where(inside, jnp.where(lane == base + j, 1.0, 0.0), own))
        lower, pivot = [], []
        for j in range(8):
            inv = 1.0 / s[j][j]
            lower.append(r[j])
            pivot.append(s[j][j])
            for i in range(8):
                if i == j:
                    continue
                f = s[i][j] * inv
                for l in range(j + 1, 8):
                    s[i][l] = s[i][l] - f * s[j][l]
                r[i] = r[i] - f * r[j]
            for l in range(j + 1, 8):
                s[j][l] = s[j][l] * inv
            r[j] = r[j] * inv
            s[j][j] = None
        out = lower[0]
        d = pivot[0]
        for j in range(1, 8):
            out = jnp.where(sub == j, lower[j], out)
            d = jnp.where(sub == j, pivot[j], d)
        keep = lane <= base + sub
        done.append(jnp.where(keep, out * lax.rsqrt(d), 0.0))
        for i in range(p + 1, n):
            t = jnp.where(inside, 0.0, rows[i])
            for l in range(8):
                t = t - jnp.broadcast_to(rows[i][:, base + l : base + l + 1], (8, M)) * r[l]
            rows[i] = t
    for p in range(n):
        work[8 * p : 8 * p + 8, :] = done[p]


PIECES = 8
PIECE = 128 * M // PIECES


def analyse(gram, anom_hbm, out_hbm, anom, out, work, in_sem, out_sem):
    def load(i):
        at = pl.ds(i * PIECE, PIECE)
        return pltpu.make_async_copy(anom_hbm.at[at], anom.at[at], in_sem.at[i])

    def store(i):
        at = pl.ds(i * PIECE, PIECE)
        return pltpu.make_async_copy(out.at[at], out_hbm.at[at], out_sem.at[i])

    for i in range(PIECES):
        load(i).start()
    inverse_factor(work, gram[...])
    transform = (math.sqrt(M - 1.0) * work[...].T).astype(BF16)
    for i in range(PIECES):
        load(i).wait()
        at = pl.ds(i * PIECE, PIECE)
        out[at, :] = jnp.dot(anom[at, :], transform, preferred_element_type=F32).astype(BF16)
        store(i).start()
    for i in range(PIECES):
        store(i).wait()


def local(anomalies, operator, local_tile_index, err_std, err_corr):
    any_spec = pl.BlockSpec(memory_space=pl.ANY)
    vmem = pl.BlockSpec(memory_space=pltpu.VMEM)
    dma = pltpu.SemaphoreType.DMA
    gram, whitened = pl.pallas_call(
        observe,
        out_shape=(jax.ShapeDtypeStruct((M, M), F32), jax.ShapeDtypeStruct((BLK, M, M), F32)),
        in_specs=[any_spec, any_spec, vmem, vmem, vmem],
        out_specs=(vmem, any_spec),
        scratch_shapes=[
            pltpu.VMEM((M, M, M), BF16),
            pltpu.VMEM((BLK, BAND, M, M), BF16),
            pltpu.VMEM((8, M), jnp.int32),
            pltpu.VMEM((BAND, 8, M), jnp.int32),
            pltpu.SMEM((BAND, 8, M), jnp.int32),
            pltpu.VMEM((BAND - 1, BLK, M, M), BF16),
            pltpu.VMEM((BAND - 1, BLK, M, M), BF16),
            pltpu.VMEM((BLK, M, M), F32),
            pltpu.VMEM((BLK, M, M), F32),
            pltpu.VMEM((M, M), F32),
            pltpu.VMEM((NEAR, ROWS + 8, M), F32),
            pltpu.VMEM((NEAR, ROWS + 8, M), F32),
            pltpu.VMEM((ROWS + 8, M), F32),
            pltpu.VMEM((FAR, ROWS + 8, M), F32),
            pltpu.VMEM((2 * NEAR, M), F32),
            pltpu.VMEM((2 * NEAR, M), F32),
            pltpu.VMEM((2 * FAR, M), F32),
            pltpu.VMEM((2 * FAR, M), F32),
            pltpu.VMEM((M, M), F32),
            pltpu.VMEM((M, M), F32),
            dma((2,)),
            dma((BAND,)),
            dma((BAND,)),
            dma((BAND,)),
            dma((BAND - 1, CHUNKS)),
            dma((BAND - 1, CHUNKS)),
            dma((NEAR,)),
            dma((NEAR,)),
            dma((FAR,)),
            dma((FAR,)),
            dma((NEAR,)),
            dma((NEAR,)),
        ],
        compiler_params=pltpu.CompilerParams(
            collective_id=0, has_side_effects=True, vmem_limit_bytes=32 * 1024 * 1024
        ),
        name="observe",
    )(
        anomalies.reshape(M, M, M),
        operator,
        local_tile_index.T,
        err_std.reshape(BLK, M),
        err_corr.reshape(BLK, M),
    )
    updated = pl.pallas_call(
        analyse,
        out_shape=jax.ShapeDtypeStruct((M * M, M), BF16),
        in_specs=[vmem, any_spec],
        out_specs=any_spec,
        scratch_shapes=[
            pltpu.VMEM((M * M, M), BF16),
            pltpu.VMEM((M * M, M), BF16),
            pltpu.VMEM((M, M), F32),
            dma((PIECES,)),
            dma((PIECES,)),
        ],
        compiler_params=pltpu.CompilerParams(vmem_limit_bytes=32 * 1024 * 1024),
        name="analyse",
    )(gram, anomalies)
    return whitened.reshape(BLK * M, M), updated


def solution(mesh):
    both = ("region", "band")
    return jax.shard_map(
        local,
        mesh=mesh,
        in_specs=(P(both, None), P(both, None, None, None), P(both, None), P(both), P(both)),
        out_specs=(P(both, None), P(both, None)),
        check_vma=False,
    )
```

```python
import functools
import math

import jax
import jax.numpy as jnp
from jax import lax
from jax.experimental import pallas as pl
from jax.experimental.pallas import tpu as pltpu
from jax.sharding import PartitionSpec as P

MESH = pl.DeviceIdType.MESH
HIGHEST = lax.Precision.HIGHEST
F32 = jnp.float32
BF16 = jnp.bfloat16

M = 128
BLK = 16
BAND = 4
CHUNK = 1
CHUNKS = BLK // CHUNK
HALF = CHUNKS // 2
NEAR = 8
FAR = 16
ROWS = M // NEAR
VMEM_BYTES = 60 * 1024 * 1024


def block_scan(decay, value):
    row = lax.broadcasted_iota(jnp.int32, (M, M), 0)
    for d in (1, 2, 4):
        seen = row >= d
        before_v = jnp.where(seen, pltpu.roll(value, d, 0), 0.0)
        before_d = jnp.where(seen, pltpu.roll(decay, d, 0), 1.0)
        value = value + decay * before_v
        decay = decay * before_d
    for d in (8, 16, 32, 64):
        value = jnp.concatenate([value[:d], value[d:] + decay[d:] * value[:-d]], axis=0)
        decay = jnp.concatenate([decay[:d], decay[d:] * decay[:-d]], axis=0)
    return decay, value


def as_columns(row):
    return jnp.broadcast_to(row, (M, M)).T


def combine(n, me, rows_at, parts, left, right, whole):
    carry = jnp.zeros((1, M), F32)
    product = jnp.ones((1, M), F32)
    cross = jnp.zeros((1, M), F32)
    square = jnp.zeros((1, M), F32)
    own_carry, own_product = carry, product
    rows = jnp.zeros((ROWS, M), F32)
    for i in range(n):
        rows = rows + parts[i, 0:ROWS]
        state = parts[i, ROWS : ROWS + 8]
        a, b, h, s = (state[k : k + 1] for k in range(4))
        mine = me == i
        own_carry = jnp.where(mine, carry, own_carry)
        own_product = jnp.where(mine, product, own_product)
        u = h + s * carry
        left[i : i + 1, :] = h
        left[n + i : n + i + 1, :] = carry
        right[i : i + 1, :] = carry
        right[n + i : n + i + 1, :] = u
        cross = cross + product * u
        square = square + product * product * s
        carry = b + a * carry
        product = product * a
    whole[...] = jnp.dot(left[...].T, right[...], precision=HIGHEST, preferred_element_type=F32)
    rows = rows + whole[pl.ds(pl.multiple_of(rows_at, ROWS), ROWS), :]
    state = jnp.concatenate([product, carry, cross, square, jnp.zeros((4, M), F32)], axis=0)
    return rows, state, own_carry, own_product


def observe(
    anom_hbm, op_hbm, idx_hbm, std_hbm, corr_hbm,
    gram_out, whit_out,
    anom, op, idx_vm, std_vm, corr_vm, idx_own, idx_in, idx, send, recv, whit, prod, gram, msg1, in1, msg2, in2, l1, r1, l2, r2, whole, gram_in,
    load_sem, idx_sem, idx_send, idx_recv, tile_send, tile_recv, s1, q1, s2, q2, s3, q3,
):
    region, band = lax.axis_index("region"), lax.axis_index("band")
    column, core = region // 2, region % 2
    near = core * BAND + band

    load_anom = pltpu.make_async_copy(anom_hbm, anom, load_sem.at[0])
    load_op = pltpu.make_async_copy(op_hbm, op, load_sem.at[1])
    load_idx = pltpu.make_async_copy(idx_hbm, idx_vm, load_sem.at[2])
    load_std = pltpu.make_async_copy(std_hbm, std_vm, load_sem.at[3])
    load_corr = pltpu.make_async_copy(corr_hbm, corr_vm, load_sem.at[4])
    load_idx.start()
    load_anom.start()
    load_std.start()
    load_corr.start()
    load_op.start()

    def near_peer(e):
        p = (near + e) % NEAR
        return (column * 2 + p // BAND, p % BAND), p

    def far_peer(e):
        q = (column + e) % FAR
        return (q * 2 + core, band), q

    barrier = pltpu.get_barrier_semaphore()
    for e in range(1, NEAR):
        pl.semaphore_signal(barrier, inc=1, device_id=near_peer(e)[0], device_id_type=MESH)
    for e in range(1, FAR):
        pl.semaphore_signal(barrier, inc=1, device_id=far_peer(e)[0], device_id_type=MESH)

    load_idx.wait()
    idx_own[...] = jnp.zeros((8, M), jnp.int32)
    idx_own[0:BAND, 0:BLK] = idx_vm[...]
    own_idx = pltpu.make_async_copy(idx_own, idx.at[0], load_sem.at[2])
    own_idx.start()
    pl.semaphore_wait(barrier, NEAR + FAR - 2)

    def idx_copy(e):
        return pltpu.make_async_remote_copy(
            src_ref=idx_own, dst_ref=idx_in.at[BAND - e], send_sem=idx_send.at[e], recv_sem=idx_recv.at[e],
            device_id=(region, (band + e) % BAND), device_id_type=MESH,
        )

    for e in (1, 3, 2):
        idx_copy(e).start()
    load_anom.wait()

    def tile_copy(k, c):
        part = pl.ds(c * CHUNK, CHUNK)
        return pltpu.make_async_remote_copy(
            src_ref=send.at[k - 1, part], dst_ref=recv.at[k - 1, part],
            send_sem=tile_send.at[k - 1, c], recv_sem=tile_recv.at[k - 1, c],
            device_id=(region, (band + BAND - k) % BAND), device_id_type=MESH,
        )

    def serve(k, c):
        for t in range(CHUNK):
            j = c * CHUNK + t
            send[k - 1, j] = anom[idx[BAND - k, k, j]]
        tile_copy(k, c).start()

    def serve_sides(c, carry):
        serve(1, c)
        serve(3, c)
        return carry

    def serve_all(c, carry):
        serve(2, c)
        serve(2, c + HALF)
        serve_sides(c + HALF, 0)
        return carry

    def to_scalar(e):
        return pltpu.make_async_copy(idx_in.at[BAND - e], idx.at[BAND - e], idx_sem.at[e])

    for e in (1, 3):
        idx_copy(e).wait_recv()
        to_scalar(e).start()
    for e in (1, 3):
        to_scalar(e).wait()
    lax.fori_loop(0, HALF, serve_sides, 0)
    idx_copy(2).wait_recv()
    to_scalar(2).start()
    to_scalar(2).wait()
    lax.fori_loop(0, HALF, serve_all, 0)
    own_idx.wait()
    load_std.wait()
    load_corr.wait()
    load_op.wait()
    gram[...] = jnp.zeros((M, M), F32)

    def use(c, carry):
        last, product, cross, square = carry
        for k in (1, 3, 2):
            tile_copy(k, c).wait_recv()
        for t in range(CHUNK):
            j = c * CHUNK + t
            value = jnp.dot(op[j, 0], anom[idx[0, 0, j]], preferred_element_type=F32)
            for k in range(1, BAND):
                value = value + jnp.dot(op[j, k], recv[k - 1, j], preferred_element_type=F32)
            value = value * as_columns(1.0 / std_vm[pl.ds(j, 1), :])
            decay, value = block_scan(as_columns(corr_vm[pl.ds(j, 1), :]), value)
            value = value + decay * last
            decay = decay * product
            whit[j] = value
            prod[j] = decay
            last, product = value[M - 1 : M], decay[M - 1 : M]
            gram[...] += jnp.dot(value.T, value, precision=HIGHEST, preferred_element_type=F32)
            cross = cross + jnp.sum(value * decay, axis=0, keepdims=True)
            square = square + jnp.sum(decay * decay, axis=0, keepdims=True)
        return last, product, cross, square

    zero = jnp.zeros((1, M), F32)
    last, product, cross, square = lax.fori_loop(0, CHUNKS, use, (zero, jnp.ones((1, M), F32), zero, zero))

    state = jnp.concatenate([product, last, cross, square, jnp.zeros((4, M), F32)], axis=0)
    for p in range(NEAR):
        msg1[p, 0:ROWS] = gram[p * ROWS : (p + 1) * ROWS]
        msg1[p, ROWS : ROWS + 8] = state

    def copy1(e):
        device, p = near_peer(e)
        return pltpu.make_async_remote_copy(
            src_ref=msg1.at[p], dst_ref=in1.at[near], send_sem=s1.at[e], recv_sem=q1.at[e],
            device_id=device, device_id_type=MESH,
        )

    for e in range(1, NEAR):
        copy1(e).start()
    in1[near] = msg1[near]
    for e in range(1, NEAR):
        copy1(e).wait_recv()
    rows, state, own_carry, own_product = combine(NEAR, near, near * ROWS, in1, l1, r1, whole)
    msg2[0:ROWS] = rows
    msg2[ROWS : ROWS + 8] = state

    def copy2(e):
        device, _ = far_peer(e)
        return pltpu.make_async_remote_copy(
            src_ref=msg2, dst_ref=in2.at[column], send_sem=s2.at[e], recv_sem=q2.at[e],
            device_id=device, device_id_type=MESH,
        )

    for e in range(1, FAR):
        copy2(e).start()
    in2[column] = msg2[...]
    for e in range(1, FAR):
        copy2(e).wait_recv()
    rows, state, far_carry, _ = combine(FAR, column, near * ROWS, in2, l2, r2, whole)
    here = lax.broadcasted_iota(jnp.int32, (ROWS, M), 0) + near * ROWS
    lane = lax.broadcasted_iota(jnp.int32, (ROWS, M), 1)
    rows = rows + jnp.where(here == lane, M - 1.0, 0.0)
    own_rows = pl.ds(pl.multiple_of(near * ROWS, ROWS), ROWS)
    gram_in[own_rows, :] = rows

    def copy3(e):
        device, _ = near_peer(e)
        return pltpu.make_async_remote_copy(
            src_ref=gram_in.at[own_rows], dst_ref=gram_in.at[own_rows], send_sem=s3.at[e], recv_sem=q3.at[e],
            device_id=device, device_id_type=MESH,
        )

    for e in range(1, NEAR):
        copy3(e).start()

    before = own_carry + own_product * far_carry

    def settle(j, carry):
        whit[j] = whit[j] + prod[j] * before
        return carry

    lax.fori_loop(0, BLK, settle, 0)
    store = pltpu.make_async_copy(whit, whit_out, load_sem.at[0])
    store.start()
    for e in range(1, NEAR):
        copy3(e).wait_recv()
    gram_out[...] = gram_in[...]

    store.wait()
    for e in (2, 1, 3):
        idx_copy(e).wait_send()

    def drain(c, carry):
        for k in range(1, BAND):
            tile_copy(k, c).wait_send()
        return carry

    lax.fori_loop(0, CHUNKS, drain, 0)
    for e in range(1, NEAR):
        copy1(e).wait_send()
        copy3(e).wait_send()
    for e in range(1, FAR):
        copy2(e).wait_send()


def inverse_factor(work, gram):
    n = M // 8
    lane = lax.broadcasted_iota(jnp.int32, (8, M), 1)
    sub = lax.broadcasted_iota(jnp.int32, (8, M), 0)
    rows = [gram[8 * i : 8 * i + 8, :] for i in range(n)]
    done = []
    for p in range(n):
        base = 8 * p
        block = rows[p]
        cols = [jnp.broadcast_to(block[:, base + l : base + l + 1], (8, M)) for l in range(8)]
        s = [[jnp.broadcast_to(cols[l][j : j + 1, :], (8, M)) for l in range(8)] for j in range(8)]
        inside = (lane >= base) & (lane < base + 8)
        r = []
        for j in range(8):
            own = jnp.broadcast_to(block[j : j + 1, :], (8, M))
            r.append(jnp.where(inside, jnp.where(lane == base + j, 1.0, 0.0), own))
        lower, pivot = [], []
        for j in range(8):
            inv = 1.0 / s[j][j]
            lower.append(r[j])
            pivot.append(s[j][j])
            for i in range(8):
                if i == j:
                    continue
                f = s[i][j] * inv
                for l in range(j + 1, 8):
                    s[i][l] = s[i][l] - f * s[j][l]
                r[i] = r[i] - f * r[j]
            for l in range(j + 1, 8):
                s[j][l] = s[j][l] * inv
            r[j] = r[j] * inv
            s[j][j] = None
        out = lower[0]
        d = pivot[0]
        for j in range(1, 8):
            out = jnp.where(sub == j, lower[j], out)
            d = jnp.where(sub == j, pivot[j], d)
        keep = lane <= base + sub
        done.append(jnp.where(keep, out * lax.rsqrt(d), 0.0))
        for i in range(p + 1, n):
            t = jnp.where(inside, 0.0, rows[i])
            for l in range(8):
                t = t - jnp.broadcast_to(rows[i][:, base + l : base + l + 1], (8, M)) * r[l]
            rows[i] = t
    for p in range(n):
        work[8 * p : 8 * p + 8, :] = done[p]


PIECES = 8
PIECE = 128 * M // PIECES


def analyse(gram, whit_hbm, anom_hbm, whit_out, out_hbm, anom, whit, out, work, in_sem, out_sem, whit_sem):
    def load(i):
        at = pl.ds(i * PIECE, PIECE)
        return pltpu.make_async_copy(anom_hbm.at[at], anom.at[at], in_sem.at[i])

    def store(i):
        at = pl.ds(i * PIECE, PIECE)
        return pltpu.make_async_copy(out.at[at], out_hbm.at[at], out_sem.at[i])

    load_whit = pltpu.make_async_copy(whit_hbm, whit, whit_sem.at[0])
    store_whit = pltpu.make_async_copy(whit, whit_out, whit_sem.at[1])
    load_whit.start()
    for i in range(PIECES):
        load(i).start()
    load_whit.wait()
    store_whit.start()
    inverse_factor(work, gram[...])
    transform = (math.sqrt(M - 1.0) * work[...].T).astype(BF16)
    for i in range(PIECES):
        load(i).wait()
        at = pl.ds(i * PIECE, PIECE)
        out[at, :] = jnp.dot(anom[at, :], transform, preferred_element_type=F32).astype(BF16)
        store(i).start()
    store_whit.wait()
    for i in range(PIECES):
        store(i).wait()


def local(anomalies, operator, local_tile_index, err_std, err_corr):
    any_spec = pl.BlockSpec(memory_space=pl.ANY)
    vmem = pl.BlockSpec(memory_space=pltpu.VMEM)
    dma = pltpu.SemaphoreType.DMA
    gram, whitened = pl.pallas_call(
        observe,
        out_shape=(jax.ShapeDtypeStruct((M, M), F32), jax.ShapeDtypeStruct((BLK, M, M), F32)),
        in_specs=[any_spec] * 5,
        out_specs=(vmem, any_spec),
        scratch_shapes=[
            pltpu.VMEM((M, M, M), BF16),
            pltpu.VMEM((BLK, BAND, M, M), BF16),
            pltpu.VMEM((BAND, BLK), jnp.int32),
            pltpu.VMEM((BLK, M), F32),
            pltpu.VMEM((BLK, M), F32),
            pltpu.VMEM((8, M), jnp.int32),
            pltpu.VMEM((BAND, 8, M), jnp.int32),
            pltpu.SMEM((BAND, 8, M), jnp.int32),
            pltpu.VMEM((BAND - 1, BLK, M, M), BF16),
            pltpu.VMEM((BAND - 1, BLK, M, M), BF16),
            pltpu.VMEM((BLK, M, M), F32),
            pltpu.VMEM((BLK, M, M), F32),
            pltpu.VMEM((M, M), F32),
            pltpu.VMEM((NEAR, ROWS + 8, M), F32),
            pltpu.VMEM((NEAR, ROWS + 8, M), F32),
            pltpu.VMEM((ROWS + 8, M), F32),
            pltpu.VMEM((FAR, ROWS + 8, M), F32),
            pltpu.VMEM((2 * NEAR, M), F32),
            pltpu.VMEM((2 * NEAR, M), F32),
            pltpu.VMEM((2 * FAR, M), F32),
            pltpu.VMEM((2 * FAR, M), F32),
            pltpu.VMEM((M, M), F32),
            pltpu.VMEM((M, M), F32),
            dma((5,)),
            dma((BAND,)),
            dma((BAND,)),
            dma((BAND,)),
            dma((BAND - 1, CHUNKS)),
            dma((BAND - 1, CHUNKS)),
            dma((NEAR,)),
            dma((NEAR,)),
            dma((FAR,)),
            dma((FAR,)),
            dma((NEAR,)),
            dma((NEAR,)),
        ],
        compiler_params=pltpu.CompilerParams(
            collective_id=0, has_side_effects=True, vmem_limit_bytes=VMEM_BYTES
        ),
        name="observe",
    )(
        anomalies.reshape(M, M, M),
        operator,
        local_tile_index.T,
        err_std.reshape(BLK, M),
        err_corr.reshape(BLK, M),
    )
    whitened, updated = pl.pallas_call(
        analyse,
        out_shape=(jax.ShapeDtypeStruct((BLK * M, M), F32), jax.ShapeDtypeStruct((M * M, M), BF16)),
        in_specs=[vmem, any_spec, any_spec],
        out_specs=(any_spec, any_spec),
        scratch_shapes=[
            pltpu.VMEM((M * M, M), BF16),
            pltpu.VMEM((BLK * M, M), F32),
            pltpu.VMEM((M * M, M), BF16),
            pltpu.VMEM((M, M), F32),
            dma((PIECES,)),
            dma((PIECES,)),
            dma((2,)),
        ],
        compiler_params=pltpu.CompilerParams(vmem_limit_bytes=VMEM_BYTES),
        name="analyse",
    )(gram, whitened.reshape(BLK * M, M), anomalies)
    return whitened, updated


def solution(mesh):
    both = ("region", "band")
    return jax.shard_map(
        local,
        mesh=mesh,
        in_specs=(P(both, None), P(both, None, None, None), P(both, None), P(both), P(both)),
        out_specs=(P(both, None), P(both, None)),
        check_vma=False,
    )
```

```python
import functools
import math

import jax
import jax.numpy as jnp
from jax import lax
from jax.experimental import pallas as pl
from jax.experimental.pallas import tpu as pltpu
from jax.sharding import PartitionSpec as P

MESH = pl.DeviceIdType.MESH
HIGHEST = lax.Precision.HIGHEST
F32 = jnp.float32
BF16 = jnp.bfloat16

M = 128
BLK = 16
BAND = 4
CHUNK = 1
CHUNKS = BLK // CHUNK
HALF = CHUNKS // 2
NEAR = 8
FAR = 16
ROWS = M // NEAR
OBSERVE_VMEM = 52 * 1024 * 1024
ANALYSE_VMEM = 16 * 1024 * 1024


def block_scan(decay, value):
    row = lax.broadcasted_iota(jnp.int32, (M, M), 0)
    for d in (1, 2, 4):
        seen = row >= d
        before_v = jnp.where(seen, pltpu.roll(value, d, 0), 0.0)
        before_d = jnp.where(seen, pltpu.roll(decay, d, 0), 1.0)
        value = value + decay * before_v
        decay = decay * before_d
    for d in (8, 16, 32, 64):
        value = jnp.concatenate([value[:d], value[d:] + decay[d:] * value[:-d]], axis=0)
        decay = jnp.concatenate([decay[:d], decay[d:] * decay[:-d]], axis=0)
    return decay, value


def as_columns(row):
    return jnp.broadcast_to(row, (M, M)).T


def combine(n, me, rows_at, parts, left, right, whole):
    carry = jnp.zeros((1, M), F32)
    product = jnp.ones((1, M), F32)
    cross = jnp.zeros((1, M), F32)
    square = jnp.zeros((1, M), F32)
    own_carry, own_product = carry, product
    rows = jnp.zeros((ROWS, M), F32)
    for i in range(n):
        rows = rows + parts[i, 0:ROWS]
        state = parts[i, ROWS : ROWS + 8]
        a, b, h, s = (state[k : k + 1] for k in range(4))
        mine = me == i
        own_carry = jnp.where(mine, carry, own_carry)
        own_product = jnp.where(mine, product, own_product)
        u = h + s * carry
        left[i : i + 1, :] = h
        left[n + i : n + i + 1, :] = carry
        right[i : i + 1, :] = carry
        right[n + i : n + i + 1, :] = u
        cross = cross + product * u
        square = square + product * product * s
        carry = b + a * carry
        product = product * a
    whole[...] = jnp.dot(left[...].T, right[...], precision=HIGHEST, preferred_element_type=F32)
    rows = rows + whole[pl.ds(pl.multiple_of(rows_at, ROWS), ROWS), :]
    state = jnp.concatenate([product, carry, cross, square, jnp.zeros((4, M), F32)], axis=0)
    return rows, state, own_carry, own_product


def observe(
    anom_hbm, op_hbm, idx_hbm, std_hbm, corr_hbm,
    gram_out, whit, anom,
    op, idx_vm, std_vm, corr_vm, idx_own, idx_in, idx, send, recv, prod, gram, msg1, in1, msg2, in2, l1, r1, l2, r2, whole, gram_in,
    load_sem, idx_sem, idx_send, idx_recv, tile_send, tile_recv, s1, q1, s2, q2, s3, q3,
):
    region, band = lax.axis_index("region"), lax.axis_index("band")
    column, core = region // 2, region % 2
    near = core * BAND + band

    load_anom = pltpu.make_async_copy(anom_hbm, anom, load_sem.at[0])
    load_op = pltpu.make_async_copy(op_hbm, op, load_sem.at[1])
    load_idx = pltpu.make_async_copy(idx_hbm, idx_vm, load_sem.at[2])
    load_std = pltpu.make_async_copy(std_hbm, std_vm, load_sem.at[3])
    load_corr = pltpu.make_async_copy(corr_hbm, corr_vm, load_sem.at[4])
    load_idx.start()
    load_anom.start()
    load_std.start()
    load_corr.start()
    load_op.start()

    def near_peer(e):
        p = (near + e) % NEAR
        return (column * 2 + p // BAND, p % BAND), p

    def far_peer(e):
        q = (column + e) % FAR
        return (q * 2 + core, band), q

    barrier = pltpu.get_barrier_semaphore()
    for e in range(1, NEAR):
        pl.semaphore_signal(barrier, inc=1, device_id=near_peer(e)[0], device_id_type=MESH)
    for e in range(1, FAR):
        pl.semaphore_signal(barrier, inc=1, device_id=far_peer(e)[0], device_id_type=MESH)

    load_idx.wait()
    idx_own[...] = jnp.zeros((8, M), jnp.int32)
    idx_own[0:BAND, 0:BLK] = idx_vm[...]
    own_idx = pltpu.make_async_copy(idx_own, idx.at[0], load_sem.at[2])
    own_idx.start()
    pl.semaphore_wait(barrier, NEAR + FAR - 2)

    def idx_copy(e):
        return pltpu.make_async_remote_copy(
            src_ref=idx_own, dst_ref=idx_in.at[BAND - e], send_sem=idx_send.at[e], recv_sem=idx_recv.at[e],
            device_id=(region, (band + e) % BAND), device_id_type=MESH,
        )

    for e in (1, 3, 2):
        idx_copy(e).start()
    load_anom.wait()

    def tile_copy(k, c):
        part = pl.ds(c * CHUNK, CHUNK)
        return pltpu.make_async_remote_copy(
            src_ref=send.at[k - 1, part], dst_ref=recv.at[k - 1, part],
            send_sem=tile_send.at[k - 1, c], recv_sem=tile_recv.at[k - 1, c],
            device_id=(region, (band + BAND - k) % BAND), device_id_type=MESH,
        )

    def serve(k, c):
        for t in range(CHUNK):
            j = c * CHUNK + t
            send[k - 1, j] = anom[idx[BAND - k, k, j]]
        tile_copy(k, c).start()

    def serve_sides(c, carry):
        serve(1, c)
        serve(3, c)
        return carry

    def serve_all(c, carry):
        serve(2, c)
        serve(2, c + HALF)
        serve_sides(c + HALF, 0)
        return carry

    def to_scalar(e):
        return pltpu.make_async_copy(idx_in.at[BAND - e], idx.at[BAND - e], idx_sem.at[e])

    for e in (1, 3):
        idx_copy(e).wait_recv()
        to_scalar(e).start()
    for e in (1, 3):
        to_scalar(e).wait()
    lax.fori_loop(0, HALF, serve_sides, 0)
    idx_copy(2).wait_recv()
    to_scalar(2).start()
    to_scalar(2).wait()
    lax.fori_loop(0, HALF, serve_all, 0)
    own_idx.wait()
    load_std.wait()
    load_corr.wait()
    load_op.wait()
    gram[...] = jnp.zeros((M, M), F32)

    def use(c, carry):
        last, product, cross, square = carry
        for k in (1, 3, 2):
            tile_copy(k, c).wait_recv()
        for t in range(CHUNK):
            j = c * CHUNK + t
            value = jnp.dot(op[j, 0], anom[idx[0, 0, j]], preferred_element_type=F32)
            for k in range(1, BAND):
                value = value + jnp.dot(op[j, k], recv[k - 1, j], preferred_element_type=F32)
            value = value * as_columns(1.0 / std_vm[pl.ds(j, 1), :])
            decay, value = block_scan(as_columns(corr_vm[pl.ds(j, 1), :]), value)
            value = value + decay * last
            decay = decay * product
            whit[j] = value
            prod[j] = decay
            last, product = value[M - 1 : M], decay[M - 1 : M]
            gram[...] += jnp.dot(value.T, value, precision=HIGHEST, preferred_element_type=F32)
            cross = cross + jnp.sum(value * decay, axis=0, keepdims=True)
            square = square + jnp.sum(decay * decay, axis=0, keepdims=True)
        return last, product, cross, square

    zero = jnp.zeros((1, M), F32)
    last, product, cross, square = lax.fori_loop(0, CHUNKS, use, (zero, jnp.ones((1, M), F32), zero, zero))

    state = jnp.concatenate([product, last, cross, square, jnp.zeros((4, M), F32)], axis=0)
    for p in range(NEAR):
        msg1[p, 0:ROWS] = gram[p * ROWS : (p + 1) * ROWS]
        msg1[p, ROWS : ROWS + 8] = state

    def copy1(e):
        device, p = near_peer(e)
        return pltpu.make_async_remote_copy(
            src_ref=msg1.at[p], dst_ref=in1.at[near], send_sem=s1.at[e], recv_sem=q1.at[e],
            device_id=device, device_id_type=MESH,
        )

    for e in range(1, NEAR):
        copy1(e).start()
    in1[near] = msg1[near]
    for e in range(1, NEAR):
        copy1(e).wait_recv()
    rows, state, own_carry, own_product = combine(NEAR, near, near * ROWS, in1, l1, r1, whole)
    msg2[0:ROWS] = rows
    msg2[ROWS : ROWS + 8] = state

    def copy2(e):
        device, _ = far_peer(e)
        return pltpu.make_async_remote_copy(
            src_ref=msg2, dst_ref=in2.at[column], send_sem=s2.at[e], recv_sem=q2.at[e],
            device_id=device, device_id_type=MESH,
        )

    for e in range(1, FAR):
        copy2(e).start()
    in2[column] = msg2[...]
    for e in range(1, FAR):
        copy2(e).wait_recv()
    rows, state, far_carry, _ = combine(FAR, column, near * ROWS, in2, l2, r2, whole)
    here = lax.broadcasted_iota(jnp.int32, (ROWS, M), 0) + near * ROWS
    lane = lax.broadcasted_iota(jnp.int32, (ROWS, M), 1)
    rows = rows + jnp.where(here == lane, M - 1.0, 0.0)
    own_rows = pl.ds(pl.multiple_of(near * ROWS, ROWS), ROWS)
    gram_in[own_rows, :] = rows

    def copy3(e):
        device, _ = near_peer(e)
        return pltpu.make_async_remote_copy(
            src_ref=gram_in.at[own_rows], dst_ref=gram_in.at[own_rows], send_sem=s3.at[e], recv_sem=q3.at[e],
            device_id=device, device_id_type=MESH,
        )

    for e in range(1, NEAR):
        copy3(e).start()

    before = own_carry + own_product * far_carry

    def settle(j, carry):
        whit[j] = whit[j] + prod[j] * before
        return carry

    lax.fori_loop(0, BLK, settle, 0)
    for e in range(1, NEAR):
        copy3(e).wait_recv()
    gram_out[...] = gram_in[...]

    for e in (2, 1, 3):
        idx_copy(e).wait_send()

    def drain(c, carry):
        for k in range(1, BAND):
            tile_copy(k, c).wait_send()
        return carry

    lax.fori_loop(0, CHUNKS, drain, 0)
    for e in range(1, NEAR):
        copy1(e).wait_send()
        copy3(e).wait_send()
    for e in range(1, FAR):
        copy2(e).wait_send()


def inverse_factor(work, gram):
    n = M // 8
    lane = lax.broadcasted_iota(jnp.int32, (8, M), 1)
    sub = lax.broadcasted_iota(jnp.int32, (8, M), 0)
    rows = [gram[8 * i : 8 * i + 8, :] for i in range(n)]
    done = []
    for p in range(n):
        base = 8 * p
        block = rows[p]
        cols = [jnp.broadcast_to(block[:, base + l : base + l + 1], (8, M)) for l in range(8)]
        s = [[jnp.broadcast_to(cols[l][j : j + 1, :], (8, M)) for l in range(8)] for j in range(8)]
        inside = (lane >= base) & (lane < base + 8)
        r = []
        for j in range(8):
            own = jnp.broadcast_to(block[j : j + 1, :], (8, M))
            r.append(jnp.where(inside, jnp.where(lane == base + j, 1.0, 0.0), own))
        lower, pivot = [], []
        for j in range(8):
            inv = 1.0 / s[j][j]
            lower.append(r[j])
            pivot.append(s[j][j])
            for i in range(8):
                if i == j:
                    continue
                f = s[i][j] * inv
                for l in range(j + 1, 8):
                    s[i][l] = s[i][l] - f * s[j][l]
                r[i] = r[i] - f * r[j]
            for l in range(j + 1, 8):
                s[j][l] = s[j][l] * inv
            r[j] = r[j] * inv
            s[j][j] = None
        out = lower[0]
        d = pivot[0]
        for j in range(1, 8):
            out = jnp.where(sub == j, lower[j], out)
            d = jnp.where(sub == j, pivot[j], d)
        keep = lane <= base + sub
        done.append(jnp.where(keep, out * lax.rsqrt(d), 0.0))
        for i in range(p + 1, n):
            t = jnp.where(inside, 0.0, rows[i])
            for l in range(8):
                t = t - jnp.broadcast_to(rows[i][:, base + l : base + l + 1], (8, M)) * r[l]
            rows[i] = t
    for p in range(n):
        work[8 * p : 8 * p + 8, :] = done[p]


PIECES = 8
PIECE = 128 * M // PIECES


def analyse(gram, whit, anom, whit_out, out_hbm, out, work, out_sem, whit_sem):
    def store(i):
        at = pl.ds(i * PIECE, PIECE)
        return pltpu.make_async_copy(out.at[at], out_hbm.at[at], out_sem.at[i])

    store_whit = pltpu.make_async_copy(whit, whit_out, whit_sem)
    store_whit.start()
    inverse_factor(work, gram[...])
    transform = (math.sqrt(M - 1.0) * work[...].T).astype(BF16)
    for i in range(PIECES):
        at = pl.ds(i * PIECE, PIECE)
        out[at, :] = jnp.dot(anom[at, :], transform, preferred_element_type=F32).astype(BF16)
        store(i).start()
    store_whit.wait()
    for i in range(PIECES):
        store(i).wait()


def local(anomalies, operator, local_tile_index, err_std, err_corr):
    any_spec = pl.BlockSpec(memory_space=pl.ANY)
    vmem = pl.BlockSpec(memory_space=pltpu.VMEM)
    dma = pltpu.SemaphoreType.DMA
    gram, whitened, held = pl.pallas_call(
        observe,
        out_shape=(
            pltpu.VMEM((M, M), F32),
            pltpu.VMEM((BLK, M, M), F32),
            pltpu.VMEM((M, M, M), BF16),
        ),
        in_specs=[any_spec] * 5,
        out_specs=(vmem, vmem, vmem),
        scratch_shapes=[
            pltpu.VMEM((BLK, BAND, M, M), BF16),
            pltpu.VMEM((BAND, BLK), jnp.int32),
            pltpu.VMEM((BLK, M), F32),
            pltpu.VMEM((BLK, M), F32),
            pltpu.VMEM((8, M), jnp.int32),
            pltpu.VMEM((BAND, 8, M), jnp.int32),
            pltpu.SMEM((BAND, 8, M), jnp.int32),
            pltpu.VMEM((BAND - 1, BLK, M, M), BF16),
            pltpu.VMEM((BAND - 1, BLK, M, M), BF16),
            pltpu.VMEM((BLK, M, M), F32),
            pltpu.VMEM((M, M), F32),
            pltpu.VMEM((NEAR, ROWS + 8, M), F32),
            pltpu.VMEM((NEAR, ROWS + 8, M), F32),
            pltpu.VMEM((ROWS + 8, M), F32),
            pltpu.VMEM((FAR, ROWS + 8, M), F32),
            pltpu.VMEM((2 * NEAR, M), F32),
            pltpu.VMEM((2 * NEAR, M), F32),
            pltpu.VMEM((2 * FAR, M), F32),
            pltpu.VMEM((2 * FAR, M), F32),
            pltpu.VMEM((M, M), F32),
            pltpu.VMEM((M, M), F32),
            dma((5,)),
            dma((BAND,)),
            dma((BAND,)),
            dma((BAND,)),
            dma((BAND - 1, CHUNKS)),
            dma((BAND - 1, CHUNKS)),
            dma((NEAR,)),
            dma((NEAR,)),
            dma((FAR,)),
            dma((FAR,)),
            dma((NEAR,)),
            dma((NEAR,)),
        ],
        compiler_params=pltpu.CompilerParams(
            collective_id=0, has_side_effects=True, vmem_limit_bytes=OBSERVE_VMEM
        ),
        name="observe",
    )(
        anomalies.reshape(M, M, M),
        operator,
        local_tile_index.T,
        err_std.reshape(BLK, M),
        err_corr.reshape(BLK, M),
    )
    whitened, updated = pl.pallas_call(
        analyse,
        out_shape=(jax.ShapeDtypeStruct((BLK * M, M), F32), jax.ShapeDtypeStruct((M * M, M), BF16)),
        in_specs=[vmem, vmem, vmem],
        out_specs=(any_spec, any_spec),
        scratch_shapes=[
            pltpu.VMEM((M * M, M), BF16),
            pltpu.VMEM((M, M), F32),
            dma((PIECES,)),
            dma,
        ],
        compiler_params=pltpu.CompilerParams(vmem_limit_bytes=ANALYSE_VMEM),
        name="analyse",
    )(gram, whitened.reshape(BLK * M, M), held.reshape(M * M, M))
    return whitened, updated


def solution(mesh):
    both = ("region", "band")
    return jax.shard_map(
        local,
        mesh=mesh,
        in_specs=(P(both, None), P(both, None, None, None), P(both, None), P(both), P(both)),
        out_specs=(P(both, None), P(both, None)),
        check_vma=False,
    )
```

```python
import functools
import math

import jax
import jax.numpy as jnp
from jax import lax
from jax.experimental import pallas as pl
from jax.experimental.pallas import tpu as pltpu
from jax.sharding import PartitionSpec as P

MESH = pl.DeviceIdType.MESH
HIGHEST = lax.Precision.HIGHEST
F32 = jnp.float32
BF16 = jnp.bfloat16

M = 128
BLK = 16
BAND = 4
CHUNK = 1
CHUNKS = BLK // CHUNK
LEAD = 2
NEAR = 8
FAR = 16
ROWS = M // NEAR
OBSERVE_VMEM = 52 * 1024 * 1024
ANALYSE_VMEM = 16 * 1024 * 1024


def block_scan(decay, value):
    row = lax.broadcasted_iota(jnp.int32, (M, M), 0)
    for d in (1, 2, 4):
        seen = row >= d
        before_v = jnp.where(seen, pltpu.roll(value, d, 0), 0.0)
        before_d = jnp.where(seen, pltpu.roll(decay, d, 0), 1.0)
        value = value + decay * before_v
        decay = decay * before_d
    for d in (8, 16, 32, 64):
        value = jnp.concatenate([value[:d], value[d:] + decay[d:] * value[:-d]], axis=0)
        decay = jnp.concatenate([decay[:d], decay[d:] * decay[:-d]], axis=0)
    return decay, value


def as_columns(row):
    return jnp.broadcast_to(row, (M, M)).T


def combine(n, me, rows_at, parts, left, right, whole):
    carry = jnp.zeros((1, M), F32)
    product = jnp.ones((1, M), F32)
    cross = jnp.zeros((1, M), F32)
    square = jnp.zeros((1, M), F32)
    own_carry, own_product = carry, product
    rows = jnp.zeros((ROWS, M), F32)
    for i in range(n):
        rows = rows + parts[i, 0:ROWS]
        state = parts[i, ROWS : ROWS + 8]
        a, b, h, s = (state[k : k + 1] for k in range(4))
        mine = me == i
        own_carry = jnp.where(mine, carry, own_carry)
        own_product = jnp.where(mine, product, own_product)
        u = h + s * carry
        left[i : i + 1, :] = h
        left[n + i : n + i + 1, :] = carry
        right[i : i + 1, :] = carry
        right[n + i : n + i + 1, :] = u
        cross = cross + product * u
        square = square + product * product * s
        carry = b + a * carry
        product = product * a
    whole[...] = jnp.dot(left[...].T, right[...], precision=HIGHEST, preferred_element_type=F32)
    rows = rows + whole[pl.ds(pl.multiple_of(rows_at, ROWS), ROWS), :]
    state = jnp.concatenate([product, carry, cross, square, jnp.zeros((4, M), F32)], axis=0)
    return rows, state, own_carry, own_product


def observe(
    anom_hbm, op_hbm, idx_hbm, std_hbm, corr_hbm,
    gram_out, whit, anom,
    op, idx_vm, std_vm, corr_vm, idx_own, idx_in, idx, send, recv, prod, gram, msg1, in1, msg2, in2, l1, r1, l2, r2, whole, gram_in,
    load_sem, idx_sem, idx_send, idx_recv, tile_send, tile_recv, s1, q1, s2, q2, s3, q3,
):
    region, band = lax.axis_index("region"), lax.axis_index("band")
    column, core = region // 2, region % 2
    near = core * BAND + band

    load_anom = pltpu.make_async_copy(anom_hbm, anom, load_sem.at[0])
    load_op = pltpu.make_async_copy(op_hbm, op, load_sem.at[1])
    load_idx = pltpu.make_async_copy(idx_hbm, idx_vm, load_sem.at[2])
    load_std = pltpu.make_async_copy(std_hbm, std_vm, load_sem.at[3])
    load_corr = pltpu.make_async_copy(corr_hbm, corr_vm, load_sem.at[4])
    load_idx.start()
    load_anom.start()
    load_std.start()
    load_corr.start()
    load_op.start()

    def near_peer(e):
        p = (near + e) % NEAR
        return (column * 2 + p // BAND, p % BAND), p

    def far_peer(e):
        q = (column + e) % FAR
        return (q * 2 + core, band), q

    barrier = pltpu.get_barrier_semaphore()
    for e in range(1, NEAR):
        pl.semaphore_signal(barrier, inc=1, device_id=near_peer(e)[0], device_id_type=MESH)
    for e in range(1, FAR):
        pl.semaphore_signal(barrier, inc=1, device_id=far_peer(e)[0], device_id_type=MESH)

    load_idx.wait()
    idx_own[...] = jnp.zeros((8, M), jnp.int32)
    idx_own[0:BAND, 0:BLK] = idx_vm[...]
    own_idx = pltpu.make_async_copy(idx_own, idx.at[0], load_sem.at[2])
    own_idx.start()
    pl.semaphore_wait(barrier, NEAR + FAR - 2)

    def idx_copy(e):
        return pltpu.make_async_remote_copy(
            src_ref=idx_own, dst_ref=idx_in.at[BAND - e], send_sem=idx_send.at[e], recv_sem=idx_recv.at[e],
            device_id=(region, (band + e) % BAND), device_id_type=MESH,
        )

    for e in (1, 3, 2):
        idx_copy(e).start()
    load_anom.wait()

    def tile_copy(k, c):
        part = pl.ds(c * CHUNK, CHUNK)
        return pltpu.make_async_remote_copy(
            src_ref=send.at[k - 1, part], dst_ref=recv.at[k - 1, part],
            send_sem=tile_send.at[k - 1, c], recv_sem=tile_recv.at[k - 1, c],
            device_id=(region, (band + BAND - k) % BAND), device_id_type=MESH,
        )

    def serve(k, c):
        for t in range(CHUNK):
            j = c * CHUNK + t
            send[k - 1, j] = anom[idx[BAND - k, k, j]]
        tile_copy(k, c).start()

    def serve_sides(c, carry):
        serve(1, c)
        serve(3, c)
        return carry

    def serve_far(c, carry):
        serve(2, c)
        return carry

    def serve_all(c, carry):
        serve(2, c)
        return serve_sides(c, carry)

    def to_scalar(e):
        return pltpu.make_async_copy(idx_in.at[BAND - e], idx.at[BAND - e], idx_sem.at[e])

    for e in (1, 3):
        idx_copy(e).wait_recv()
        to_scalar(e).start()
    for e in (1, 3):
        to_scalar(e).wait()
    lax.fori_loop(0, LEAD, serve_sides, 0)
    idx_copy(2).wait_recv()
    to_scalar(2).start()
    to_scalar(2).wait()
    lax.fori_loop(0, LEAD, serve_far, 0)
    lax.fori_loop(LEAD, CHUNKS, serve_all, 0)
    own_idx.wait()
    load_std.wait()
    load_corr.wait()
    load_op.wait()
    gram[...] = jnp.zeros((M, M), F32)

    def use(c, carry):
        last, product, cross, square = carry
        for k in (1, 3, 2):
            tile_copy(k, c).wait_recv()
        for t in range(CHUNK):
            j = c * CHUNK + t
            value = jnp.dot(op[j, 0], anom[idx[0, 0, j]], preferred_element_type=F32)
            for k in range(1, BAND):
                value = value + jnp.dot(op[j, k], recv[k - 1, j], preferred_element_type=F32)
            value = value * as_columns(1.0 / std_vm[pl.ds(j, 1), :])
            decay, value = block_scan(as_columns(corr_vm[pl.ds(j, 1), :]), value)
            value = value + decay * last
            decay = decay * product
            whit[j] = value
            prod[j] = decay
            last, product = value[M - 1 : M], decay[M - 1 : M]
            gram[...] += jnp.dot(value.T, value, precision=HIGHEST, preferred_element_type=F32)
            cross = cross + jnp.sum(value * decay, axis=0, keepdims=True)
            square = square + jnp.sum(decay * decay, axis=0, keepdims=True)
        return last, product, cross, square

    zero = jnp.zeros((1, M), F32)
    last, product, cross, square = lax.fori_loop(0, CHUNKS, use, (zero, jnp.ones((1, M), F32), zero, zero))

    state = jnp.concatenate([product, last, cross, square, jnp.zeros((4, M), F32)], axis=0)
    for p in range(NEAR):
        msg1[p, 0:ROWS] = gram[p * ROWS : (p + 1) * ROWS]
        msg1[p, ROWS : ROWS + 8] = state

    def copy1(e):
        device, p = near_peer(e)
        return pltpu.make_async_remote_copy(
            src_ref=msg1.at[p], dst_ref=in1.at[near], send_sem=s1.at[e], recv_sem=q1.at[e],
            device_id=device, device_id_type=MESH,
        )

    for e in range(1, NEAR):
        copy1(e).start()
    in1[near] = msg1[near]
    for e in range(1, NEAR):
        copy1(e).wait_recv()
    rows, state, own_carry, own_product = combine(NEAR, near, near * ROWS, in1, l1, r1, whole)
    msg2[0:ROWS] = rows
    msg2[ROWS : ROWS + 8] = state

    def copy2(e):
        device, _ = far_peer(e)
        return pltpu.make_async_remote_copy(
            src_ref=msg2, dst_ref=in2.at[column], send_sem=s2.at[e], recv_sem=q2.at[e],
            device_id=device, device_id_type=MESH,
        )

    for e in range(1, FAR):
        copy2(e).start()
    in2[column] = msg2[...]
    for e in range(1, FAR):
        copy2(e).wait_recv()
    rows, state, far_carry, _ = combine(FAR, column, near * ROWS, in2, l2, r2, whole)
    here = lax.broadcasted_iota(jnp.int32, (ROWS, M), 0) + near * ROWS
    lane = lax.broadcasted_iota(jnp.int32, (ROWS, M), 1)
    rows = rows + jnp.where(here == lane, M - 1.0, 0.0)
    own_rows = pl.ds(pl.multiple_of(near * ROWS, ROWS), ROWS)
    gram_in[own_rows, :] = rows

    def copy3(e):
        device, _ = near_peer(e)
        return pltpu.make_async_remote_copy(
            src_ref=gram_in.at[own_rows], dst_ref=gram_in.at[own_rows], send_sem=s3.at[e], recv_sem=q3.at[e],
            device_id=device, device_id_type=MESH,
        )

    for e in range(1, NEAR):
        copy3(e).start()

    before = own_carry + own_product * far_carry

    def settle(j, carry):
        whit[j] = whit[j] + prod[j] * before
        return carry

    lax.fori_loop(0, BLK, settle, 0)
    for e in range(1, NEAR):
        copy3(e).wait_recv()
    gram_out[...] = gram_in[...]

    for e in (2, 1, 3):
        idx_copy(e).wait_send()

    def drain(c, carry):
        for k in range(1, BAND):
            tile_copy(k, c).wait_send()
        return carry

    lax.fori_loop(0, CHUNKS, drain, 0)
    for e in range(1, NEAR):
        copy1(e).wait_send()
        copy3(e).wait_send()
    for e in range(1, FAR):
        copy2(e).wait_send()


def inverse_factor(work, gram):
    n = M // 8
    lane = lax.broadcasted_iota(jnp.int32, (8, M), 1)
    sub = lax.broadcasted_iota(jnp.int32, (8, M), 0)
    rows = [gram[8 * i : 8 * i + 8, :] for i in range(n)]
    done = []
    for p in range(n):
        base = 8 * p
        block = rows[p]
        cols = [jnp.broadcast_to(block[:, base + l : base + l + 1], (8, M)) for l in range(8)]
        s = [[jnp.broadcast_to(cols[l][j : j + 1, :], (8, M)) for l in range(8)] for j in range(8)]
        inside = (lane >= base) & (lane < base + 8)
        r = []
        for j in range(8):
            own = jnp.broadcast_to(block[j : j + 1, :], (8, M))
            r.append(jnp.where(inside, jnp.where(lane == base + j, 1.0, 0.0), own))
        lower, pivot = [], []
        for j in range(8):
            inv = 1.0 / s[j][j]
            lower.append(r[j])
            pivot.append(s[j][j])
            for i in range(8):
                if i == j:
                    continue
                f = s[i][j] * inv
                for l in range(j + 1, 8):
                    s[i][l] = s[i][l] - f * s[j][l]
                r[i] = r[i] - f * r[j]
            for l in range(j + 1, 8):
                s[j][l] = s[j][l] * inv
            r[j] = r[j] * inv
            s[j][j] = None
        out = lower[0]
        d = pivot[0]
        for j in range(1, 8):
            out = jnp.where(sub == j, lower[j], out)
            d = jnp.where(sub == j, pivot[j], d)
        keep = lane <= base + sub
        done.append(jnp.where(keep, out * lax.rsqrt(d), 0.0))
        for i in range(p + 1, n):
            t = jnp.where(inside, 0.0, rows[i])
            for l in range(8):
                t = t - jnp.broadcast_to(rows[i][:, base + l : base + l + 1], (8, M)) * r[l]
            rows[i] = t
    for p in range(n):
        work[8 * p : 8 * p + 8, :] = done[p]


PIECES = 8
PIECE = 128 * M // PIECES


def analyse(gram, whit, anom, whit_out, out_hbm, out, work, out_sem, whit_sem):
    def store(i):
        at = pl.ds(i * PIECE, PIECE)
        return pltpu.make_async_copy(out.at[at], out_hbm.at[at], out_sem.at[i])

    store_whit = pltpu.make_async_copy(whit, whit_out, whit_sem)
    store_whit.start()
    inverse_factor(work, gram[...])
    transform = (math.sqrt(M - 1.0) * work[...].T).astype(BF16)
    for i in range(PIECES):
        at = pl.ds(i * PIECE, PIECE)
        out[at, :] = jnp.dot(anom[at, :], transform, preferred_element_type=F32).astype(BF16)
        store(i).start()
    store_whit.wait()
    for i in range(PIECES):
        store(i).wait()


def local(anomalies, operator, local_tile_index, err_std, err_corr):
    any_spec = pl.BlockSpec(memory_space=pl.ANY)
    vmem = pl.BlockSpec(memory_space=pltpu.VMEM)
    dma = pltpu.SemaphoreType.DMA
    gram, whitened, held = pl.pallas_call(
        observe,
        out_shape=(
            pltpu.VMEM((M, M), F32),
            pltpu.VMEM((BLK, M, M), F32),
            pltpu.VMEM((M, M, M), BF16),
        ),
        in_specs=[any_spec] * 5,
        out_specs=(vmem, vmem, vmem),
        scratch_shapes=[
            pltpu.VMEM((BLK, BAND, M, M), BF16),
            pltpu.VMEM((BAND, BLK), jnp.int32),
            pltpu.VMEM((BLK, M), F32),
            pltpu.VMEM((BLK, M), F32),
            pltpu.VMEM((8, M), jnp.int32),
            pltpu.VMEM((BAND, 8, M), jnp.int32),
            pltpu.SMEM((BAND, 8, M), jnp.int32),
            pltpu.VMEM((BAND - 1, BLK, M, M), BF16),
            pltpu.VMEM((BAND - 1, BLK, M, M), BF16),
            pltpu.VMEM((BLK, M, M), F32),
            pltpu.VMEM((M, M), F32),
            pltpu.VMEM((NEAR, ROWS + 8, M), F32),
            pltpu.VMEM((NEAR, ROWS + 8, M), F32),
            pltpu.VMEM((ROWS + 8, M), F32),
            pltpu.VMEM((FAR, ROWS + 8, M), F32),
            pltpu.VMEM((2 * NEAR, M), F32),
            pltpu.VMEM((2 * NEAR, M), F32),
            pltpu.VMEM((2 * FAR, M), F32),
            pltpu.VMEM((2 * FAR, M), F32),
            pltpu.VMEM((M, M), F32),
            pltpu.VMEM((M, M), F32),
            dma((5,)),
            dma((BAND,)),
            dma((BAND,)),
            dma((BAND,)),
            dma((BAND - 1, CHUNKS)),
            dma((BAND - 1, CHUNKS)),
            dma((NEAR,)),
            dma((NEAR,)),
            dma((FAR,)),
            dma((FAR,)),
            dma((NEAR,)),
            dma((NEAR,)),
        ],
        compiler_params=pltpu.CompilerParams(
            collective_id=0, has_side_effects=True, vmem_limit_bytes=OBSERVE_VMEM
        ),
        name="observe",
    )(
        anomalies.reshape(M, M, M),
        operator,
        local_tile_index.T,
        err_std.reshape(BLK, M),
        err_corr.reshape(BLK, M),
    )
    whitened, updated = pl.pallas_call(
        analyse,
        out_shape=(jax.ShapeDtypeStruct((BLK * M, M), F32), jax.ShapeDtypeStruct((M * M, M), BF16)),
        in_specs=[vmem, vmem, vmem],
        out_specs=(any_spec, any_spec),
        scratch_shapes=[
            pltpu.VMEM((M * M, M), BF16),
            pltpu.VMEM((M, M), F32),
            dma((PIECES,)),
            dma,
        ],
        compiler_params=pltpu.CompilerParams(vmem_limit_bytes=ANALYSE_VMEM),
        name="analyse",
    )(gram, whitened.reshape(BLK * M, M), held.reshape(M * M, M))
    return whitened, updated


def solution(mesh):
    both = ("region", "band")
    return jax.shard_map(
        local,
        mesh=mesh,
        in_specs=(P(both, None), P(both, None, None, None), P(both, None), P(both), P(both)),
        out_specs=(P(both, None), P(both, None)),
        check_vma=False,
    )
```

```python
import functools
import math

import jax
import jax.numpy as jnp
from jax import lax
from jax.experimental import pallas as pl
from jax.experimental.pallas import tpu as pltpu
from jax.sharding import PartitionSpec as P

MESH = pl.DeviceIdType.MESH
HIGHEST = lax.Precision.HIGHEST
F32 = jnp.float32
BF16 = jnp.bfloat16

M = 128
BLK = 16
BAND = 4
CHUNK = 1
CHUNKS = BLK // CHUNK
LEAD = 2
NEAR = 8
FAR = 16
ROWS = M // NEAR
OBSERVE_VMEM = 52 * 1024 * 1024
ANALYSE_VMEM = 16 * 1024 * 1024


def block_scan(decay, value):
    row = lax.broadcasted_iota(jnp.int32, (M, M), 0)
    for d in (1, 2, 4):
        seen = row >= d
        before_v = jnp.where(seen, pltpu.roll(value, d, 0), 0.0)
        before_d = jnp.where(seen, pltpu.roll(decay, d, 0), 1.0)
        value = value + decay * before_v
        decay = decay * before_d
    for d in (8, 16, 32, 64):
        value = jnp.concatenate([value[:d], value[d:] + decay[d:] * value[:-d]], axis=0)
        decay = jnp.concatenate([decay[:d], decay[d:] * decay[:-d]], axis=0)
    return decay, value


def as_columns(row):
    return jnp.broadcast_to(row, (M, M)).T


def combine(n, me, rows_at, parts, left, right):
    carry = jnp.zeros((1, M), F32)
    product = jnp.ones((1, M), F32)
    cross = jnp.zeros((1, M), F32)
    square = jnp.zeros((1, M), F32)
    own_carry, own_product = carry, product
    rows = jnp.zeros((ROWS, M), F32)
    for i in range(n):
        rows = rows + parts[i, 0:ROWS]
        state = parts[i, ROWS : ROWS + 8]
        a, b, h, s = (state[k : k + 1] for k in range(4))
        mine = me == i
        own_carry = jnp.where(mine, carry, own_carry)
        own_product = jnp.where(mine, product, own_product)
        u = h + s * carry
        left[i : i + 1, :] = h
        left[n + i : n + i + 1, :] = carry
        right[i : i + 1, :] = carry
        right[n + i : n + i + 1, :] = u
        cross = cross + product * u
        square = square + product * product * s
        carry = b + a * carry
        product = product * a
    own = pltpu.roll(left[...], (M - rows_at) % M, 1)[:, 0:ROWS]
    rows = rows + jnp.dot(own.T, right[...], precision=HIGHEST, preferred_element_type=F32)
    state = jnp.concatenate([product, carry, cross, square, jnp.zeros((4, M), F32)], axis=0)
    return rows, state, own_carry, own_product


def observe(
    anom_hbm, op_hbm, idx_hbm, std_hbm, corr_hbm,
    gram_out, whit, anom,
    op, idx_vm, std_vm, corr_vm, idx_own, idx_in, idx, send, recv, prod, gram, msg1, in1, msg2, in2, l1, r1, l2, r2, gram_in,
    load_sem, idx_sem, idx_send, idx_recv, tile_send, tile_recv, s1, q1, s2, q2, s3, q3,
):
    region, band = lax.axis_index("region"), lax.axis_index("band")
    column, core = region // 2, region % 2
    near = core * BAND + band

    load_anom = pltpu.make_async_copy(anom_hbm, anom, load_sem.at[0])
    load_op = pltpu.make_async_copy(op_hbm, op, load_sem.at[1])
    load_idx = pltpu.make_async_copy(idx_hbm, idx_vm, load_sem.at[2])
    load_std = pltpu.make_async_copy(std_hbm, std_vm, load_sem.at[3])
    load_corr = pltpu.make_async_copy(corr_hbm, corr_vm, load_sem.at[4])
    load_idx.start()

    def near_peer(e):
        p = (near + e) % NEAR
        return (column * 2 + p // BAND, p % BAND), p

    def far_peer(e):
        q = (column + e) % FAR
        return (q * 2 + core, band), q

    barrier = pltpu.get_barrier_semaphore()
    for e in range(1, NEAR):
        pl.semaphore_signal(barrier, inc=1, device_id=near_peer(e)[0], device_id_type=MESH)
    for e in range(1, FAR):
        pl.semaphore_signal(barrier, inc=1, device_id=far_peer(e)[0], device_id_type=MESH)

    load_anom.start()
    load_std.start()
    load_corr.start()
    load_op.start()
    load_idx.wait()
    idx_own[...] = jnp.zeros((8, M), jnp.int32)
    idx_own[0:BAND, 0:BLK] = idx_vm[...]
    own_idx = pltpu.make_async_copy(idx_own, idx.at[0], load_sem.at[2])
    own_idx.start()
    pl.semaphore_wait(barrier, NEAR + FAR - 2)

    def idx_copy(e):
        return pltpu.make_async_remote_copy(
            src_ref=idx_own, dst_ref=idx_in.at[BAND - e], send_sem=idx_send.at[e], recv_sem=idx_recv.at[e],
            device_id=(region, (band + e) % BAND), device_id_type=MESH,
        )

    for e in (1, 3, 2):
        idx_copy(e).start()
    load_anom.wait()

    def tile_copy(k, c):
        part = pl.ds(c * CHUNK, CHUNK)
        return pltpu.make_async_remote_copy(
            src_ref=send.at[k - 1, part], dst_ref=recv.at[k - 1, part],
            send_sem=tile_send.at[k - 1, c], recv_sem=tile_recv.at[k - 1, c],
            device_id=(region, (band + BAND - k) % BAND), device_id_type=MESH,
        )

    def serve(k, c):
        for t in range(CHUNK):
            j = c * CHUNK + t
            send[k - 1, j] = anom[idx[BAND - k, k, j]]
        tile_copy(k, c).start()

    def serve_first(k, c):
        for t in range(CHUNK):
            j = c * CHUNK + t
            send[k - 1, j] = anom[idx_in[BAND - k, k : k + 1, :][0, j]]
        tile_copy(k, c).start()

    def serve_sides(c, carry):
        serve(1, c)
        serve(3, c)
        return carry

    def serve_far(c, carry):
        serve(2, c)
        return carry

    def serve_all(c, carry):
        serve(2, c)
        return serve_sides(c, carry)

    def to_scalar(e):
        return pltpu.make_async_copy(idx_in.at[BAND - e], idx.at[BAND - e], idx_sem.at[e])

    for e in (1, 3):
        idx_copy(e).wait_recv()
        to_scalar(e).start()
    for c in range(LEAD):
        for k in (1, 3):
            serve_first(k, c)
    for e in (1, 3):
        to_scalar(e).wait()
    idx_copy(2).wait_recv()
    to_scalar(2).start()
    to_scalar(2).wait()
    lax.fori_loop(0, LEAD, serve_far, 0)
    lax.fori_loop(LEAD, CHUNKS, serve_all, 0)
    own_idx.wait()
    load_std.wait()
    load_corr.wait()
    load_op.wait()
    gram[...] = jnp.zeros((M, M), F32)

    def use(c, carry):
        last, product, cross, square = carry
        for k in (1, 3, 2):
            tile_copy(k, c).wait_recv()
        for t in range(CHUNK):
            j = c * CHUNK + t
            value = jnp.dot(op[j, 0], anom[idx[0, 0, j]], preferred_element_type=F32)
            for k in range(1, BAND):
                value = value + jnp.dot(op[j, k], recv[k - 1, j], preferred_element_type=F32)
            value = value * as_columns(1.0 / std_vm[pl.ds(j, 1), :])
            decay, value = block_scan(as_columns(corr_vm[pl.ds(j, 1), :]), value)
            value = value + decay * last
            decay = decay * product
            whit[j] = value
            prod[j] = decay
            last, product = value[M - 1 : M], decay[M - 1 : M]
            gram[...] += jnp.dot(value.T, value, precision=HIGHEST, preferred_element_type=F32)
            cross = cross + jnp.sum(value * decay, axis=0, keepdims=True)
            square = square + jnp.sum(decay * decay, axis=0, keepdims=True)
        return last, product, cross, square

    zero = jnp.zeros((1, M), F32)
    last, product, cross, square = lax.fori_loop(0, CHUNKS, use, (zero, jnp.ones((1, M), F32), zero, zero))

    state = jnp.concatenate([product, last, cross, square, jnp.zeros((4, M), F32)], axis=0)
    for p in range(NEAR):
        msg1[p, 0:ROWS] = gram[p * ROWS : (p + 1) * ROWS]
        msg1[p, ROWS : ROWS + 8] = state

    def copy1(e):
        device, p = near_peer(e)
        return pltpu.make_async_remote_copy(
            src_ref=msg1.at[p], dst_ref=in1.at[near], send_sem=s1.at[e], recv_sem=q1.at[e],
            device_id=device, device_id_type=MESH,
        )

    for e in range(1, NEAR):
        copy1(e).start()
    in1[near] = msg1[near]

    def drain(c, carry):
        for k in range(1, BAND):
            tile_copy(k, c).wait_send()
        return carry

    lax.fori_loop(0, CHUNKS, drain, 0)
    for e in (2, 1, 3):
        idx_copy(e).wait_send()
    for e in range(1, NEAR):
        copy1(e).wait_recv()
    rows, state, own_carry, own_product = combine(NEAR, near, near * ROWS, in1, l1, r1)
    msg2[0:ROWS] = rows
    msg2[ROWS : ROWS + 8] = state

    def copy2(e):
        device, _ = far_peer(e)
        return pltpu.make_async_remote_copy(
            src_ref=msg2, dst_ref=in2.at[column], send_sem=s2.at[e], recv_sem=q2.at[e],
            device_id=device, device_id_type=MESH,
        )

    for e in range(1, FAR):
        copy2(e).start()
    in2[column] = msg2[...]
    for e in range(1, NEAR):
        copy1(e).wait_send()
    for e in range(1, FAR):
        copy2(e).wait_recv()
    rows, state, far_carry, _ = combine(FAR, column, near * ROWS, in2, l2, r2)
    here = lax.broadcasted_iota(jnp.int32, (ROWS, M), 0) + near * ROWS
    lane = lax.broadcasted_iota(jnp.int32, (ROWS, M), 1)
    rows = rows + jnp.where(here == lane, M - 1.0, 0.0)
    own_rows = pl.ds(pl.multiple_of(near * ROWS, ROWS), ROWS)
    gram_in[own_rows, :] = rows

    def copy3(e):
        device, _ = near_peer(e)
        return pltpu.make_async_remote_copy(
            src_ref=gram_in.at[own_rows], dst_ref=gram_in.at[own_rows], send_sem=s3.at[e], recv_sem=q3.at[e],
            device_id=device, device_id_type=MESH,
        )

    for e in range(1, NEAR):
        copy3(e).start()

    before = own_carry + own_product * far_carry

    def settle(j, carry):
        whit[j] = whit[j] + prod[j] * before
        return carry

    lax.fori_loop(0, BLK, settle, 0)
    for e in range(1, FAR):
        copy2(e).wait_send()
    for e in range(1, NEAR):
        copy3(e).wait_recv()
    gram_out[...] = gram_in[...]

    for e in range(1, NEAR):
        copy3(e).wait_send()


def inverse_factor(work, gram):
    n = M // 8
    lane = lax.broadcasted_iota(jnp.int32, (8, M), 1)
    sub = lax.broadcasted_iota(jnp.int32, (8, M), 0)
    rows = [gram[8 * i : 8 * i + 8, :] for i in range(n)]
    for p in range(n):
        base = 8 * p
        block = rows[p]
        cols = [jnp.broadcast_to(block[:, base + l : base + l + 1], (8, M)) for l in range(8)]
        s = {(j, l): jnp.broadcast_to(cols[l][j : j + 1, :], (8, M)) for l in range(8) for j in range(l + 1)}
        inside = (lane >= base) & (lane < base + 8)
        r = []
        for j in range(8):
            own = jnp.broadcast_to(block[j : j + 1, :], (8, M))
            r.append(jnp.where(inside, jnp.where(lane == base + j, 1.0, 0.0), own))
        lower, pivot = [], []
        for j in range(8):
            inv = 1.0 / s[j, j]
            lower.append(r[j])
            pivot.append(s[j, j])
            for i in range(8):
                if i == j:
                    continue
                f = (s[j, i] if i > j else s[i, j]) * inv
                for l in range(max(i, j + 1), 8):
                    s[i, l] = s[i, l] - f * s[j, l]
                r[i] = r[i] - f * r[j]
            for l in range(j + 1, 8):
                s[j, l] = s[j, l] * inv
            r[j] = r[j] * inv
        out, d = lower[0], pivot[0]
        for j in range(1, 8):
            out = jnp.where(sub == j, lower[j], out)
            d = jnp.where(sub == j, pivot[j], d)
        keep = lane <= base + sub
        work[8 * p : 8 * p + 8, :] = jnp.where(keep, out * lax.rsqrt(d), 0.0)
        for i in range(p + 1, n):
            t = jnp.where(inside, 0.0, rows[i])
            for l in range(8):
                t = t - jnp.broadcast_to(rows[i][:, base + l : base + l + 1], (8, M)) * r[l]
            rows[i] = t


PIECES = 16
PIECE = 128 * M // PIECES


def analyse(gram, whit, anom, whit_out, out_hbm, out, work, out_sem, whit_sem):
    def store(i):
        at = pl.ds(i * PIECE, PIECE)
        return pltpu.make_async_copy(out.at[at], out_hbm.at[at], out_sem.at[i])

    store_whit = pltpu.make_async_copy(whit, whit_out, whit_sem)
    store_whit.start()
    inverse_factor(work, gram[...])
    transform = (math.sqrt(M - 1.0) * work[...].T).astype(BF16)
    for i in range(PIECES):
        at = pl.ds(i * PIECE, PIECE)
        out[at, :] = jnp.dot(anom[at, :], transform, preferred_element_type=F32).astype(BF16)
        store(i).start()
    store_whit.wait()
    for i in range(PIECES):
        store(i).wait()


def local(anomalies, operator, local_tile_index, err_std, err_corr):
    any_spec = pl.BlockSpec(memory_space=pl.ANY)
    vmem = pl.BlockSpec(memory_space=pltpu.VMEM)
    dma = pltpu.SemaphoreType.DMA
    gram, whitened, held = pl.pallas_call(
        observe,
        out_shape=(
            pltpu.VMEM((M, M), F32),
            pltpu.VMEM((BLK, M, M), F32),
            pltpu.VMEM((M, M, M), BF16),
        ),
        in_specs=[any_spec] * 5,
        out_specs=(vmem, vmem, vmem),
        scratch_shapes=[
            pltpu.VMEM((BLK, BAND, M, M), BF16),
            pltpu.VMEM((BAND, BLK), jnp.int32),
            pltpu.VMEM((BLK, M), F32),
            pltpu.VMEM((BLK, M), F32),
            pltpu.VMEM((8, M), jnp.int32),
            pltpu.VMEM((BAND, 8, M), jnp.int32),
            pltpu.SMEM((BAND, 8, M), jnp.int32),
            pltpu.VMEM((BAND - 1, BLK, M, M), BF16),
            pltpu.VMEM((BAND - 1, BLK, M, M), BF16),
            pltpu.VMEM((BLK, M, M), F32),
            pltpu.VMEM((M, M), F32),
            pltpu.VMEM((NEAR, ROWS + 8, M), F32),
            pltpu.VMEM((NEAR, ROWS + 8, M), F32),
            pltpu.VMEM((ROWS + 8, M), F32),
            pltpu.VMEM((FAR, ROWS + 8, M), F32),
            pltpu.VMEM((2 * NEAR, M), F32),
            pltpu.VMEM((2 * NEAR, M), F32),
            pltpu.VMEM((2 * FAR, M), F32),
            pltpu.VMEM((2 * FAR, M), F32),
            pltpu.VMEM((M, M), F32),
            dma((5,)),
            dma((BAND,)),
            dma((BAND,)),
            dma((BAND,)),
            dma((BAND - 1, CHUNKS)),
            dma((BAND - 1, CHUNKS)),
            dma((NEAR,)),
            dma((NEAR,)),
            dma((FAR,)),
            dma((FAR,)),
            dma((NEAR,)),
            dma((NEAR,)),
        ],
        compiler_params=pltpu.CompilerParams(
            collective_id=0, has_side_effects=True, vmem_limit_bytes=OBSERVE_VMEM
        ),
        name="observe",
    )(
        anomalies.reshape(M, M, M),
        operator,
        local_tile_index.T,
        err_std.reshape(BLK, M),
        err_corr.reshape(BLK, M),
    )
    whitened, updated = pl.pallas_call(
        analyse,
        out_shape=(jax.ShapeDtypeStruct((BLK * M, M), F32), jax.ShapeDtypeStruct((M * M, M), BF16)),
        in_specs=[vmem, vmem, vmem],
        out_specs=(any_spec, any_spec),
        scratch_shapes=[
            pltpu.VMEM((M * M, M), BF16),
            pltpu.VMEM((M, M), F32),
            dma((PIECES,)),
            dma,
        ],
        compiler_params=pltpu.CompilerParams(vmem_limit_bytes=ANALYSE_VMEM),
        name="analyse",
    )(gram, whitened.reshape(BLK * M, M), held.reshape(M * M, M))
    return whitened, updated


def solution(mesh):
    both = ("region", "band")
    return jax.shard_map(
        local,
        mesh=mesh,
        in_specs=(P(both, None), P(both, None, None, None), P(both, None), P(both), P(both)),
        out_specs=(P(both, None), P(both, None)),
        check_vma=False,
    )
```

```python
import functools
import math

import jax
import jax.numpy as jnp
from jax import lax
from jax.experimental import pallas as pl
from jax.experimental.pallas import tpu as pltpu
from jax.sharding import PartitionSpec as P

MESH = pl.DeviceIdType.MESH
HIGHEST = lax.Precision.HIGHEST
F32 = jnp.float32
BF16 = jnp.bfloat16

M = 128
BLK = 16
BAND = 4
CHUNK = 1
CHUNKS = BLK // CHUNK
LEAD = 2
NEAR = 8
FAR = 16
NEAR_ORDER = (6, 2, 5, 7, 1, 3, 4)
FAR_ORDER = (10, 6, 9, 11, 14, 2, 5, 7, 8, 13, 15, 1, 3, 4, 12)
ROWS = M // NEAR
OBSERVE_VMEM = 52 * 1024 * 1024
ANALYSE_VMEM = 16 * 1024 * 1024


def block_scan(decay, value):
    row = lax.broadcasted_iota(jnp.int32, (M, M), 0)
    for d in (1, 2, 4):
        seen = row >= d
        before_v = jnp.where(seen, pltpu.roll(value, d, 0), 0.0)
        before_d = jnp.where(seen, pltpu.roll(decay, d, 0), 1.0)
        value = value + decay * before_v
        decay = decay * before_d
    for d in (8, 16, 32, 64):
        value = jnp.concatenate([value[:d], value[d:] + decay[d:] * value[:-d]], axis=0)
        decay = jnp.concatenate([decay[:d], decay[d:] * decay[:-d]], axis=0)
    return decay, value


def as_columns(row):
    return jnp.broadcast_to(row, (M, M)).T


def combine(n, me, rows_at, parts, left, right):
    carry = jnp.zeros((1, M), F32)
    product = jnp.ones((1, M), F32)
    cross = jnp.zeros((1, M), F32)
    square = jnp.zeros((1, M), F32)
    own_carry, own_product = carry, product
    rows = jnp.zeros((ROWS, M), F32)
    for i in range(n):
        rows = rows + parts[i, 0:ROWS]
        state = parts[i, ROWS : ROWS + 4]
        a, b, h, s = (state[k : k + 1] for k in range(4))
        mine = me == i
        own_carry = jnp.where(mine, carry, own_carry)
        own_product = jnp.where(mine, product, own_product)
        u = h + s * carry
        left[i : i + 1, :] = h
        left[n + i : n + i + 1, :] = carry
        right[i : i + 1, :] = carry
        right[n + i : n + i + 1, :] = u
        cross = cross + product * u
        square = square + product * product * s
        carry = b + a * carry
        product = product * a
    own = pltpu.roll(left[...], (M - rows_at) % M, 1)[:, 0:ROWS]
    rows = rows + jnp.dot(own.T, right[...], precision=HIGHEST, preferred_element_type=F32)
    state = jnp.concatenate([product, carry, cross, square], axis=0)
    return rows, state, own_carry, own_product


def observe(
    anom_hbm, op_hbm, idx_hbm, std_hbm, corr_hbm,
    gram_out, whit, anom,
    op, idx_vm, std_vm, corr_vm, idx_own, idx_in, idx, send, recv, prod, gram, msg1, in1, msg2, in2, l1, r1, l2, r2, gram_in,
    load_sem, idx_sem, idx_send, idx_recv, tile_send, tile_recv, s1, q1, s2, q2, s3, q3,
):
    region, band = lax.axis_index("region"), lax.axis_index("band")
    column, core = region // 2, region % 2
    near = core * BAND + band

    load_anom = pltpu.make_async_copy(anom_hbm, anom, load_sem.at[0])
    load_op = pltpu.make_async_copy(op_hbm, op, load_sem.at[1])
    load_idx = pltpu.make_async_copy(idx_hbm, idx_vm, load_sem.at[2])
    load_std = pltpu.make_async_copy(std_hbm, std_vm, load_sem.at[3])
    load_corr = pltpu.make_async_copy(corr_hbm, corr_vm, load_sem.at[4])
    load_idx.start()

    def near_peer(e):
        p = (core + e // BAND) % 2 * BAND + (band + e % BAND) % BAND
        return (column * 2 + p // BAND, p % BAND), p

    def far_peer(e):
        q = (column // 4 + e // 4) % 4 * 4 + (column % 4 + e % 4) % 4
        return (q * 2 + core, band), q

    barrier = pltpu.get_barrier_semaphore()
    for e in range(1, NEAR):
        pl.semaphore_signal(barrier, inc=1, device_id=near_peer(e)[0], device_id_type=MESH)
    for e in range(1, FAR):
        pl.semaphore_signal(barrier, inc=1, device_id=far_peer(e)[0], device_id_type=MESH)

    load_anom.start()
    load_std.start()
    load_corr.start()
    load_op.start()
    load_idx.wait()
    idx_own[...] = jnp.zeros((8, M), jnp.int32)
    idx_own[0:BAND, 0:BLK] = idx_vm[...]
    own_idx = pltpu.make_async_copy(idx_own, idx.at[0], load_sem.at[2])
    own_idx.start()
    pl.semaphore_wait(barrier, NEAR + FAR - 2)

    def idx_copy(e):
        return pltpu.make_async_remote_copy(
            src_ref=idx_own, dst_ref=idx_in.at[BAND - e], send_sem=idx_send.at[e], recv_sem=idx_recv.at[e],
            device_id=(region, (band + e) % BAND), device_id_type=MESH,
        )

    for e in (1, 3, 2):
        idx_copy(e).start()
    load_anom.wait()

    def tile_copy(k, c):
        part = pl.ds(c * CHUNK, CHUNK)
        return pltpu.make_async_remote_copy(
            src_ref=send.at[k - 1, part], dst_ref=recv.at[k - 1, part],
            send_sem=tile_send.at[k - 1, c], recv_sem=tile_recv.at[k - 1, c],
            device_id=(region, (band + BAND - k) % BAND), device_id_type=MESH,
        )

    def serve(k, c):
        for t in range(CHUNK):
            j = c * CHUNK + t
            send[k - 1, j] = anom[idx[BAND - k, k, j]]
        tile_copy(k, c).start()

    def serve_first(k, c):
        for t in range(CHUNK):
            j = c * CHUNK + t
            send[k - 1, j] = anom[idx_in[BAND - k, k : k + 1, :][0, j]]
        tile_copy(k, c).start()

    def serve_sides(c, carry):
        serve(1, c)
        serve(3, c)
        return carry

    def serve_far(c, carry):
        serve(2, c)
        return carry

    def serve_all(c, carry):
        serve(2, c)
        return serve_sides(c, carry)

    def to_scalar(e):
        return pltpu.make_async_copy(idx_in.at[BAND - e], idx.at[BAND - e], idx_sem.at[e])

    for e in (1, 3):
        idx_copy(e).wait_recv()
        to_scalar(e).start()
    for c in range(LEAD):
        for k in (1, 3):
            serve_first(k, c)
    for e in (1, 3):
        to_scalar(e).wait()
    idx_copy(2).wait_recv()
    to_scalar(2).start()
    to_scalar(2).wait()
    lax.fori_loop(0, LEAD, serve_far, 0)
    lax.fori_loop(LEAD, CHUNKS, serve_all, 0)
    own_idx.wait()
    load_std.wait()
    load_corr.wait()
    load_op.wait()
    gram[...] = jnp.zeros((M, M), F32)

    def use(c, carry):
        last, product, cross, square = carry
        for k in (1, 3, 2):
            tile_copy(k, c).wait_recv()
        for t in range(CHUNK):
            j = c * CHUNK + t
            value = jnp.dot(op[j, 0], anom[idx[0, 0, j]], preferred_element_type=F32)
            for k in range(1, BAND):
                value = value + jnp.dot(op[j, k], recv[k - 1, j], preferred_element_type=F32)
            value = value * as_columns(1.0 / std_vm[pl.ds(j, 1), :])
            decay, value = block_scan(as_columns(corr_vm[pl.ds(j, 1), :]), value)
            value = value + decay * last
            decay = decay * product
            whit[j] = value
            prod[j] = decay
            last, product = value[M - 1 : M], decay[M - 1 : M]
            gram[...] += jnp.dot(value.T, value, precision=HIGHEST, preferred_element_type=F32)
            cross = cross + jnp.sum(value * decay, axis=0, keepdims=True)
            square = square + jnp.sum(decay * decay, axis=0, keepdims=True)
        return last, product, cross, square

    zero = jnp.zeros((1, M), F32)
    last, product, cross, square = lax.fori_loop(0, CHUNKS, use, (zero, jnp.ones((1, M), F32), zero, zero))

    state = jnp.concatenate([product, last, cross, square], axis=0)
    for p in range(NEAR):
        msg1[p, 0:ROWS] = gram[p * ROWS : (p + 1) * ROWS]
        msg1[p, ROWS : ROWS + 4] = state

    def copy1(e):
        device, p = near_peer(e)
        return pltpu.make_async_remote_copy(
            src_ref=msg1.at[p], dst_ref=in1.at[near], send_sem=s1.at[e], recv_sem=q1.at[e],
            device_id=device, device_id_type=MESH,
        )

    for e in NEAR_ORDER:
        copy1(e).start()
    in1[near] = msg1[near]

    def drain(c, carry):
        for k in range(1, BAND):
            tile_copy(k, c).wait_send()
        return carry

    lax.fori_loop(0, CHUNKS, drain, 0)
    for e in (2, 1, 3):
        idx_copy(e).wait_send()
    for e in range(1, NEAR):
        copy1(e).wait_recv()
    rows, state, own_carry, own_product = combine(NEAR, near, near * ROWS, in1, l1, r1)
    msg2[0:ROWS] = rows
    msg2[ROWS : ROWS + 4] = state

    def copy2(e):
        device, _ = far_peer(e)
        return pltpu.make_async_remote_copy(
            src_ref=msg2, dst_ref=in2.at[column], send_sem=s2.at[e], recv_sem=q2.at[e],
            device_id=device, device_id_type=MESH,
        )

    for e in FAR_ORDER:
        copy2(e).start()
    in2[column] = msg2[...]
    for e in range(1, NEAR):
        copy1(e).wait_send()
    for e in range(1, FAR):
        copy2(e).wait_recv()
    rows, state, far_carry, _ = combine(FAR, column, near * ROWS, in2, l2, r2)
    here = lax.broadcasted_iota(jnp.int32, (ROWS, M), 0) + near * ROWS
    lane = lax.broadcasted_iota(jnp.int32, (ROWS, M), 1)
    rows = rows + jnp.where(here == lane, M - 1.0, 0.0)
    own_rows = pl.ds(pl.multiple_of(near * ROWS, ROWS), ROWS)
    gram_in[own_rows, :] = rows

    def copy3(e):
        device, _ = near_peer(e)
        return pltpu.make_async_remote_copy(
            src_ref=gram_in.at[own_rows], dst_ref=gram_in.at[own_rows], send_sem=s3.at[e], recv_sem=q3.at[e],
            device_id=device, device_id_type=MESH,
        )

    for e in NEAR_ORDER:
        copy3(e).start()

    before = own_carry + own_product * far_carry

    def settle(j, carry):
        whit[j] = whit[j] + prod[j] * before
        return carry

    lax.fori_loop(0, BLK, settle, 0)
    for e in range(1, FAR):
        copy2(e).wait_send()
    for e in range(1, NEAR):
        copy3(e).wait_recv()
    gram_out[...] = gram_in[...]

    for e in range(1, NEAR):
        copy3(e).wait_send()


def inverse_factor(work, gram, spread):
    n = M // 8
    lane = lax.broadcasted_iota(jnp.int32, (8, M), 1)
    sub = lax.broadcasted_iota(jnp.int32, (8, M), 0)
    rows = [gram[8 * i : 8 * i + 8, :] for i in range(n)]
    for p in range(n):
        base = 8 * p
        block = rows[p]
        cols = [jnp.broadcast_to(block[:, base + l : base + l + 1], (8, M)) for l in range(8)]
        side = p % 2 * 64
        for l in range(8):
            spread[side + 8 * l : side + 8 * l + 8, :] = cols[l]
        s = {}
        for l in range(8):
            for j in range(l + 1):
                at = side + 8 * l + j
                s[j, l] = jnp.broadcast_to(spread[at : at + 1, :], (8, M))
        inside = (lane >= base) & (lane < base + 8)
        r = []
        for j in range(8):
            own = jnp.broadcast_to(block[j : j + 1, :], (8, M))
            r.append(jnp.where(inside, jnp.where(lane == base + j, 1.0, 0.0), own))
        lower, pivot = [], []
        for j in range(8):
            inv = 1.0 / s[j, j]
            lower.append(r[j])
            pivot.append(s[j, j])
            for i in range(8):
                if i == j:
                    continue
                f = (s[j, i] if i > j else s[i, j]) * inv
                for l in range(max(i, j + 1), 8):
                    s[i, l] = s[i, l] - f * s[j, l]
                r[i] = r[i] - f * r[j]
            for l in range(j + 1, 8):
                s[j, l] = s[j, l] * inv
            r[j] = r[j] * inv
        out, d = lower[0], pivot[0]
        for j in range(1, 8):
            out = jnp.where(sub == j, lower[j], out)
            d = jnp.where(sub == j, pivot[j], d)
        keep = lane <= base + sub
        work[8 * p : 8 * p + 8, :] = jnp.where(keep, out * lax.rsqrt(d), 0.0)
        for i in range(p + 1, n):
            t = jnp.where(inside, 0.0, rows[i])
            for l in range(8):
                t = t - jnp.broadcast_to(rows[i][:, base + l : base + l + 1], (8, M)) * r[l]
            rows[i] = t


PIECES = 16
PIECE = 128 * M // PIECES


def analyse(gram, whit, anom, whit_out, out_hbm, out, work, spread, out_sem, whit_sem):
    def store(i):
        at = pl.ds(i * PIECE, PIECE)
        return pltpu.make_async_copy(out.at[at], out_hbm.at[at], out_sem.at[i])

    store_whit = pltpu.make_async_copy(whit, whit_out, whit_sem)
    store_whit.start()
    inverse_factor(work, gram[...], spread)
    transform = (math.sqrt(M - 1.0) * work[...].T).astype(BF16)
    for i in range(PIECES):
        at = pl.ds(i * PIECE, PIECE)
        out[at, :] = jnp.dot(anom[at, :], transform, preferred_element_type=F32).astype(BF16)
        store(i).start()
    store_whit.wait()
    for i in range(PIECES):
        store(i).wait()


def local(anomalies, operator, local_tile_index, err_std, err_corr):
    any_spec = pl.BlockSpec(memory_space=pl.ANY)
    vmem = pl.BlockSpec(memory_space=pltpu.VMEM)
    dma = pltpu.SemaphoreType.DMA
    gram, whitened, held = pl.pallas_call(
        observe,
        out_shape=(
            pltpu.VMEM((M, M), F32),
            pltpu.VMEM((BLK, M, M), F32),
            pltpu.VMEM((M, M, M), BF16),
        ),
        in_specs=[any_spec] * 5,
        out_specs=(vmem, vmem, vmem),
        scratch_shapes=[
            pltpu.VMEM((BLK, BAND, M, M), BF16),
            pltpu.VMEM((BAND, BLK), jnp.int32),
            pltpu.VMEM((BLK, M), F32),
            pltpu.VMEM((BLK, M), F32),
            pltpu.VMEM((8, M), jnp.int32),
            pltpu.VMEM((BAND, 8, M), jnp.int32),
            pltpu.SMEM((BAND, 8, M), jnp.int32),
            pltpu.VMEM((BAND - 1, BLK, M, M), BF16),
            pltpu.VMEM((BAND - 1, BLK, M, M), BF16),
            pltpu.VMEM((BLK, M, M), F32),
            pltpu.VMEM((M, M), F32),
            pltpu.VMEM((NEAR, ROWS + 4, M), F32),
            pltpu.VMEM((NEAR, ROWS + 4, M), F32),
            pltpu.VMEM((ROWS + 4, M), F32),
            pltpu.VMEM((FAR, ROWS + 4, M), F32),
            pltpu.VMEM((2 * NEAR, M), F32),
            pltpu.VMEM((2 * NEAR, M), F32),
            pltpu.VMEM((2 * FAR, M), F32),
            pltpu.VMEM((2 * FAR, M), F32),
            pltpu.VMEM((M, M), F32),
            dma((5,)),
            dma((BAND,)),
            dma((BAND,)),
            dma((BAND,)),
            dma((BAND - 1, CHUNKS)),
            dma((BAND - 1, CHUNKS)),
            dma((NEAR,)),
            dma((NEAR,)),
            dma((FAR,)),
            dma((FAR,)),
            dma((NEAR,)),
            dma((NEAR,)),
        ],
        compiler_params=pltpu.CompilerParams(
            collective_id=0, has_side_effects=True, vmem_limit_bytes=OBSERVE_VMEM
        ),
        name="observe",
    )(
        anomalies.reshape(M, M, M),
        operator,
        local_tile_index.T,
        err_std.reshape(BLK, M),
        err_corr.reshape(BLK, M),
    )
    whitened, updated = pl.pallas_call(
        analyse,
        out_shape=(jax.ShapeDtypeStruct((BLK * M, M), F32), jax.ShapeDtypeStruct((M * M, M), BF16)),
        in_specs=[vmem, vmem, vmem],
        out_specs=(any_spec, any_spec),
        scratch_shapes=[
            pltpu.VMEM((M * M, M), BF16),
            pltpu.VMEM((M, M), F32),
            pltpu.VMEM((2 * 64, M), F32),
            dma((PIECES,)),
            dma,
        ],
        compiler_params=pltpu.CompilerParams(vmem_limit_bytes=ANALYSE_VMEM),
        name="analyse",
    )(gram, whitened.reshape(BLK * M, M), held.reshape(M * M, M))
    return whitened, updated


def solution(mesh):
    both = ("region", "band")
    return jax.shard_map(
        local,
        mesh=mesh,
        in_specs=(P(both, None), P(both, None, None, None), P(both, None), P(both), P(both)),
        out_specs=(P(both, None), P(both, None)),
        check_vma=False,
    )
```

```python
import functools
import math

import jax
import jax.numpy as jnp
from jax import lax
from jax.experimental import pallas as pl
from jax.experimental.pallas import tpu as pltpu
from jax.sharding import PartitionSpec as P

MESH = pl.DeviceIdType.MESH
HIGHEST = lax.Precision.HIGHEST
F32 = jnp.float32
BF16 = jnp.bfloat16

M = 128
BLK = 16
BAND = 4
CHUNK = 1
CHUNKS = BLK // CHUNK
LEAD = 2
NEAR = 8
FAR = 16
NEAR_ORDER = (6, 2, 5, 7, 1, 3, 4)
FAR_ORDER = (10, 6, 9, 11, 14, 2, 5, 7, 8, 13, 15, 1, 3, 4, 12)
ROWS = M // NEAR
OBSERVE_VMEM = 52 * 1024 * 1024
ANALYSE_VMEM = 16 * 1024 * 1024


def block_scan(decay, value):
    row = lax.broadcasted_iota(jnp.int32, (M, M), 0)
    for d in (1, 2, 4):
        seen = row >= d
        before_v = jnp.where(seen, pltpu.roll(value, d, 0), 0.0)
        before_d = jnp.where(seen, pltpu.roll(decay, d, 0), 1.0)
        value = value + decay * before_v
        decay = decay * before_d
    for d in (8, 16, 32, 64):
        value = jnp.concatenate([value[:d], value[d:] + decay[d:] * value[:-d]], axis=0)
        decay = jnp.concatenate([decay[:d], decay[d:] * decay[:-d]], axis=0)
    return decay, value


def as_columns(row):
    return jnp.broadcast_to(row, (M, M)).T


def combine(n, me, rows_at, parts, left, right):
    carry = jnp.zeros((1, M), F32)
    product = jnp.ones((1, M), F32)
    cross = jnp.zeros((1, M), F32)
    square = jnp.zeros((1, M), F32)
    own_carry, own_product = carry, product
    rows = jnp.zeros((ROWS, M), F32)
    for i in range(n):
        rows = rows + parts[i, 0:ROWS]
        state = parts[i, ROWS : ROWS + 4]
        a, b, h, s = (state[k : k + 1] for k in range(4))
        mine = me == i
        own_carry = jnp.where(mine, carry, own_carry)
        own_product = jnp.where(mine, product, own_product)
        u = h + s * carry
        left[i : i + 1, :] = h
        left[n + i : n + i + 1, :] = carry
        right[i : i + 1, :] = carry
        right[n + i : n + i + 1, :] = u
        cross = cross + product * u
        square = square + product * product * s
        carry = b + a * carry
        product = product * a
    own = pltpu.roll(left[...], (M - rows_at) % M, 1)[:, 0:ROWS]
    rows = rows + jnp.dot(own.T, right[...], precision=HIGHEST, preferred_element_type=F32)
    state = jnp.concatenate([product, carry, cross, square], axis=0)
    return rows, state, own_carry, own_product


def observe(
    anom_hbm, op_hbm, idx_hbm, std_hbm, corr_hbm,
    gram_out, whit, anom,
    op, idx_vm, std_vm, corr_vm, idx_own, idx_in, idx, send, recv, prod, gram, msg1, in1, msg2, in2, l1, r1, l2, r2, gram_in,
    load_sem, idx_sem, idx_send, idx_recv, tile_send, tile_recv, s1, q1, s2, q2, s3, q3,
):
    region, band = lax.axis_index("region"), lax.axis_index("band")
    column, core = region // 2, region % 2
    near = core * BAND + band

    load_anom = pltpu.make_async_copy(anom_hbm, anom, load_sem.at[0])
    load_op = pltpu.make_async_copy(op_hbm, op, load_sem.at[1])
    load_idx = pltpu.make_async_copy(idx_hbm, idx_vm, load_sem.at[2])
    load_std = pltpu.make_async_copy(std_hbm, std_vm, load_sem.at[3])
    load_corr = pltpu.make_async_copy(corr_hbm, corr_vm, load_sem.at[4])
    load_idx.start()

    def near_peer(e):
        p = (core + e // BAND) % 2 * BAND + (band + e % BAND) % BAND
        return (column * 2 + p // BAND, p % BAND), p

    def far_peer(e):
        q = (column // 4 + e // 4) % 4 * 4 + (column % 4 + e % 4) % 4
        return (q * 2 + core, band), q

    barrier = pltpu.get_barrier_semaphore()
    for e in range(1, NEAR):
        pl.semaphore_signal(barrier, inc=1, device_id=near_peer(e)[0], device_id_type=MESH)
    for e in range(1, FAR):
        pl.semaphore_signal(barrier, inc=1, device_id=far_peer(e)[0], device_id_type=MESH)

    load_anom.start()
    load_std.start()
    load_corr.start()
    load_op.start()
    load_idx.wait()
    idx_own[...] = jnp.zeros((8, M), jnp.int32)
    idx_own[0:BAND, 0:BLK] = idx_vm[...]
    own_idx = pltpu.make_async_copy(idx_own, idx.at[0], load_sem.at[2])
    own_idx.start()
    pl.semaphore_wait(barrier, NEAR + FAR - 2)

    def idx_copy(e):
        return pltpu.make_async_remote_copy(
            src_ref=idx_own, dst_ref=idx_in.at[BAND - e], send_sem=idx_send.at[e], recv_sem=idx_recv.at[e],
            device_id=(region, (band + e) % BAND), device_id_type=MESH,
        )

    for e in (1, 3, 2):
        idx_copy(e).start()
    load_anom.wait()

    def tile_copy(k, c):
        part = pl.ds(c * CHUNK, CHUNK)
        return pltpu.make_async_remote_copy(
            src_ref=send.at[k - 1, part], dst_ref=recv.at[k - 1, part],
            send_sem=tile_send.at[k - 1, c], recv_sem=tile_recv.at[k - 1, c],
            device_id=(region, (band + BAND - k) % BAND), device_id_type=MESH,
        )

    def serve(k, c):
        for t in range(CHUNK):
            j = c * CHUNK + t
            send[k - 1, j] = anom[idx[BAND - k, k, j]]
        tile_copy(k, c).start()

    def serve_first(k, c):
        for t in range(CHUNK):
            j = c * CHUNK + t
            send[k - 1, j] = anom[idx_in[BAND - k, k : k + 1, :][0, j]]
        tile_copy(k, c).start()

    def serve_sides(c, carry):
        serve(1, c)
        serve(3, c)
        return carry

    def serve_all(c, carry):
        serve(2, c)
        return serve_sides(c, carry)

    def to_scalar(e):
        return pltpu.make_async_copy(idx_in.at[BAND - e], idx.at[BAND - e], idx_sem.at[e])

    for e in (1, 3):
        idx_copy(e).wait_recv()
        to_scalar(e).start()
    for c in range(LEAD):
        for k in (1, 3):
            serve_first(k, c)
    for e in (1, 3):
        to_scalar(e).wait()
    idx_copy(2).wait_recv()
    to_scalar(2).start()
    for c in range(LEAD):
        serve_first(2, c)
    to_scalar(2).wait()
    lax.fori_loop(LEAD, CHUNKS, serve_all, 0)
    own_idx.wait()
    load_std.wait()
    load_corr.wait()
    load_op.wait()
    gram[...] = jnp.zeros((M, M), F32)

    def use(c, carry):
        last, product, cross, square = carry
        for k in (1, 3, 2):
            tile_copy(k, c).wait_recv()
        for t in range(CHUNK):
            j = c * CHUNK + t
            value = jnp.dot(op[j, 0], anom[idx[0, 0, j]], preferred_element_type=F32)
            for k in range(1, BAND):
                value = value + jnp.dot(op[j, k], recv[k - 1, j], preferred_element_type=F32)
            value = value * as_columns(1.0 / std_vm[pl.ds(j, 1), :])
            decay, value = block_scan(as_columns(corr_vm[pl.ds(j, 1), :]), value)
            value = value + decay * last
            decay = decay * product
            whit[j] = value
            prod[j] = decay
            last, product = value[M - 1 : M], decay[M - 1 : M]
            gram[...] += jnp.dot(value.T, value, precision=HIGHEST, preferred_element_type=F32)
            cross = cross + jnp.sum(value * decay, axis=0, keepdims=True)
            square = square + jnp.sum(decay * decay, axis=0, keepdims=True)
        return last, product, cross, square

    zero = jnp.zeros((1, M), F32)
    last, product, cross, square = lax.fori_loop(0, CHUNKS, use, (zero, jnp.ones((1, M), F32), zero, zero))

    state = jnp.concatenate([product, last, cross, square], axis=0)
    for p in range(NEAR):
        msg1[p, 0:ROWS] = gram[p * ROWS : (p + 1) * ROWS]
        msg1[p, ROWS : ROWS + 4] = state

    def copy1(e):
        device, p = near_peer(e)
        return pltpu.make_async_remote_copy(
            src_ref=msg1.at[p], dst_ref=in1.at[near], send_sem=s1.at[e], recv_sem=q1.at[e],
            device_id=device, device_id_type=MESH,
        )

    for e in NEAR_ORDER:
        copy1(e).start()
    in1[near] = msg1[near]

    def drain(c, carry):
        for k in range(1, BAND):
            tile_copy(k, c).wait_send()
        return carry

    lax.fori_loop(0, CHUNKS, drain, 0)
    for e in (2, 1, 3):
        idx_copy(e).wait_send()
    for e in range(1, NEAR):
        copy1(e).wait_recv()
    rows, state, own_carry, own_product = combine(NEAR, near, near * ROWS, in1, l1, r1)
    msg2[0:ROWS] = rows
    msg2[ROWS : ROWS + 4] = state

    def copy2(e):
        device, _ = far_peer(e)
        return pltpu.make_async_remote_copy(
            src_ref=msg2, dst_ref=in2.at[column], send_sem=s2.at[e], recv_sem=q2.at[e],
            device_id=device, device_id_type=MESH,
        )

    for e in FAR_ORDER:
        copy2(e).start()
    in2[column] = msg2[...]
    for e in range(1, NEAR):
        copy1(e).wait_send()
    for e in range(1, FAR):
        copy2(e).wait_recv()
    rows, state, far_carry, _ = combine(FAR, column, near * ROWS, in2, l2, r2)
    here = lax.broadcasted_iota(jnp.int32, (ROWS, M), 0) + near * ROWS
    lane = lax.broadcasted_iota(jnp.int32, (ROWS, M), 1)
    rows = rows + jnp.where(here == lane, M - 1.0, 0.0)
    own_rows = pl.ds(pl.multiple_of(near * ROWS, ROWS), ROWS)
    gram_in[own_rows, :] = rows

    def copy3(e):
        device, _ = near_peer(e)
        return pltpu.make_async_remote_copy(
            src_ref=gram_in.at[own_rows], dst_ref=gram_in.at[own_rows], send_sem=s3.at[e], recv_sem=q3.at[e],
            device_id=device, device_id_type=MESH,
        )

    for e in NEAR_ORDER:
        copy3(e).start()

    before = own_carry + own_product * far_carry

    def settle(j, carry):
        whit[j] = whit[j] + prod[j] * before
        return carry

    lax.fori_loop(0, BLK, settle, 0)
    for e in range(1, FAR):
        copy2(e).wait_send()
    for e in range(1, NEAR):
        copy3(e).wait_recv()
    gram_out[...] = gram_in[...]

    for e in range(1, NEAR):
        copy3(e).wait_send()


def inverse_factor(work, gram, spread):
    n = M // 8
    lane = lax.broadcasted_iota(jnp.int32, (8, M), 1)
    sub = lax.broadcasted_iota(jnp.int32, (8, M), 0)
    rows = [gram[8 * i : 8 * i + 8, :] for i in range(n)]
    for p in range(n):
        base = 8 * p
        block = rows[p]
        cols = [jnp.broadcast_to(block[:, base + l : base + l + 1], (8, M)) for l in range(8)]
        side = p % 2 * 64
        for l in range(8):
            spread[side + 8 * l : side + 8 * l + 8, :] = cols[l]
        s = {}
        for l in range(8):
            for j in range(l + 1):
                at = side + 8 * l + j
                s[j, l] = jnp.broadcast_to(spread[at : at + 1, :], (8, M))
        inside = (lane >= base) & (lane < base + 8)
        r = []
        for j in range(8):
            own = jnp.broadcast_to(block[j : j + 1, :], (8, M))
            r.append(jnp.where(inside, jnp.where(lane == base + j, 1.0, 0.0), own))
        lower, pivot = [], []
        for j in range(8):
            inv = 1.0 / s[j, j]
            lower.append(r[j])
            pivot.append(s[j, j])
            for i in range(8):
                if i == j:
                    continue
                f = (s[j, i] if i > j else s[i, j]) * inv
                for l in range(max(i, j + 1), 8):
                    s[i, l] = s[i, l] - f * s[j, l]
                r[i] = r[i] - f * r[j]
            for l in range(j + 1, 8):
                s[j, l] = s[j, l] * inv
            r[j] = r[j] * inv
        out, d = lower[0], pivot[0]
        for j in range(1, 8):
            out = jnp.where(sub == j, lower[j], out)
            d = jnp.where(sub == j, pivot[j], d)
        keep = lane <= base + sub
        work[8 * p : 8 * p + 8, :] = jnp.where(keep, out * lax.rsqrt(d), 0.0)
        for i in range(p + 1, n):
            terms = [jnp.broadcast_to(rows[i][:, base + l : base + l + 1], (8, M)) * r[l] for l in range(8)]
            while len(terms) > 1:
                terms = [a + b for a, b in zip(terms[0::2], terms[1::2])]
            rows[i] = jnp.where(inside, 0.0, rows[i]) - terms[0]


PIECES = 16
PIECE = 128 * M // PIECES


def analyse(gram, whit, anom, whit_out, out_hbm, out, work, spread, out_sem, whit_sem):
    def store(i):
        at = pl.ds(i * PIECE, PIECE)
        return pltpu.make_async_copy(out.at[at], out_hbm.at[at], out_sem.at[i])

    store_whit = pltpu.make_async_copy(whit, whit_out, whit_sem)
    store_whit.start()
    inverse_factor(work, gram[...], spread)
    transform = (math.sqrt(M - 1.0) * work[...].T).astype(BF16)
    for i in range(PIECES):
        at = pl.ds(i * PIECE, PIECE)
        out[at, :] = jnp.dot(anom[at, :], transform, preferred_element_type=F32).astype(BF16)
        store(i).start()
    store_whit.wait()
    for i in range(PIECES):
        store(i).wait()


def local(anomalies, operator, local_tile_index, err_std, err_corr):
    any_spec = pl.BlockSpec(memory_space=pl.ANY)
    vmem = pl.BlockSpec(memory_space=pltpu.VMEM)
    dma = pltpu.SemaphoreType.DMA
    gram, whitened, held = pl.pallas_call(
        observe,
        out_shape=(
            pltpu.VMEM((M, M), F32),
            pltpu.VMEM((BLK, M, M), F32),
            pltpu.VMEM((M, M, M), BF16),
        ),
        in_specs=[any_spec] * 5,
        out_specs=(vmem, vmem, vmem),
        scratch_shapes=[
            pltpu.VMEM((BLK, BAND, M, M), BF16),
            pltpu.VMEM((BAND, BLK), jnp.int32),
            pltpu.VMEM((BLK, M), F32),
            pltpu.VMEM((BLK, M), F32),
            pltpu.VMEM((8, M), jnp.int32),
            pltpu.VMEM((BAND, 8, M), jnp.int32),
            pltpu.SMEM((BAND, 8, M), jnp.int32),
            pltpu.VMEM((BAND - 1, BLK, M, M), BF16),
            pltpu.VMEM((BAND - 1, BLK, M, M), BF16),
            pltpu.VMEM((BLK, M, M), F32),
            pltpu.VMEM((M, M), F32),
            pltpu.VMEM((NEAR, ROWS + 4, M), F32),
            pltpu.VMEM((NEAR, ROWS + 4, M), F32),
            pltpu.VMEM((ROWS + 4, M), F32),
            pltpu.VMEM((FAR, ROWS + 4, M), F32),
            pltpu.VMEM((2 * NEAR, M), F32),
            pltpu.VMEM((2 * NEAR, M), F32),
            pltpu.VMEM((2 * FAR, M), F32),
            pltpu.VMEM((2 * FAR, M), F32),
            pltpu.VMEM((M, M), F32),
            dma((5,)),
            dma((BAND,)),
            dma((BAND,)),
            dma((BAND,)),
            dma((BAND - 1, CHUNKS)),
            dma((BAND - 1, CHUNKS)),
            dma((NEAR,)),
            dma((NEAR,)),
            dma((FAR,)),
            dma((FAR,)),
            dma((NEAR,)),
            dma((NEAR,)),
        ],
        compiler_params=pltpu.CompilerParams(
            collective_id=0, has_side_effects=True, vmem_limit_bytes=OBSERVE_VMEM
        ),
        name="observe",
    )(
        anomalies.reshape(M, M, M),
        operator,
        local_tile_index.T,
        err_std.reshape(BLK, M),
        err_corr.reshape(BLK, M),
    )
    whitened, updated = pl.pallas_call(
        analyse,
        out_shape=(jax.ShapeDtypeStruct((BLK * M, M), F32), jax.ShapeDtypeStruct((M * M, M), BF16)),
        in_specs=[vmem, vmem, vmem],
        out_specs=(any_spec, any_spec),
        scratch_shapes=[
            pltpu.VMEM((M * M, M), BF16),
            pltpu.VMEM((M, M), F32),
            pltpu.VMEM((2 * 64, M), F32),
            dma((PIECES,)),
            dma,
        ],
        compiler_params=pltpu.CompilerParams(vmem_limit_bytes=ANALYSE_VMEM),
        name="analyse",
    )(gram, whitened.reshape(BLK * M, M), held.reshape(M * M, M))
    return whitened, updated


def solution(mesh):
    both = ("region", "band")
    return jax.shard_map(
        local,
        mesh=mesh,
        in_specs=(P(both, None), P(both, None, None, None), P(both, None), P(both), P(both)),
        out_specs=(P(both, None), P(both, None)),
        check_vma=False,
    )
```

```python
import functools
import math

import jax
import jax.numpy as jnp
from jax import lax
from jax.experimental import pallas as pl
from jax.experimental.pallas import tpu as pltpu
from jax.sharding import PartitionSpec as P

MESH = pl.DeviceIdType.MESH
HIGHEST = lax.Precision.HIGHEST
F32 = jnp.float32
BF16 = jnp.bfloat16

M = 128
BLK = 16
BAND = 4
CHUNK = 1
CHUNKS = BLK // CHUNK
LEAD = 2
NEAR = 8
FAR = 16
NEAR_ORDER = (6, 2, 5, 7, 1, 3, 4)
FAR_ORDER = (10, 6, 9, 11, 14, 2, 5, 7, 8, 13, 15, 1, 3, 4, 12)
ROWS = M // NEAR
OBSERVE_VMEM = 52 * 1024 * 1024
ANALYSE_VMEM = 16 * 1024 * 1024


def block_scan(decay, value):
    row = lax.broadcasted_iota(jnp.int32, (M, M), 0)
    for d in (1, 2, 4):
        seen = row >= d
        before_v = jnp.where(seen, pltpu.roll(value, d, 0), 0.0)
        before_d = jnp.where(seen, pltpu.roll(decay, d, 0), 1.0)
        value = value + decay * before_v
        decay = decay * before_d
    for d in (8, 16, 32, 64):
        value = jnp.concatenate([value[:d], value[d:] + decay[d:] * value[:-d]], axis=0)
        decay = jnp.concatenate([decay[:d], decay[d:] * decay[:-d]], axis=0)
    return decay, value


def as_columns(row):
    return jnp.broadcast_to(row, (M, M)).T


def combine(n, me, rows_at, parts, left, right):
    carry = jnp.zeros((1, M), F32)
    product = jnp.ones((1, M), F32)
    cross = jnp.zeros((1, M), F32)
    square = jnp.zeros((1, M), F32)
    own_carry, own_product = carry, product
    rows = jnp.zeros((ROWS, M), F32)
    for i in range(n):
        rows = rows + parts[i, 0:ROWS]
        state = parts[i, ROWS : ROWS + 4]
        a, b, h, s = (state[k : k + 1] for k in range(4))
        mine = me == i
        own_carry = jnp.where(mine, carry, own_carry)
        own_product = jnp.where(mine, product, own_product)
        u = h + s * carry
        left[i : i + 1, :] = h
        left[n + i : n + i + 1, :] = carry
        right[i : i + 1, :] = carry
        right[n + i : n + i + 1, :] = u
        cross = cross + product * u
        square = square + product * product * s
        carry = b + a * carry
        product = product * a
    own = pltpu.roll(left[...], (M - rows_at) % M, 1)[:, 0:ROWS]
    rows = rows + jnp.dot(own.T, right[...], precision=HIGHEST, preferred_element_type=F32)
    state = jnp.concatenate([product, carry, cross, square], axis=0)
    return rows, state, own_carry, own_product


def observe(
    anom_hbm, op_hbm, idx_hbm, std_hbm, corr_hbm,
    gram_out, whit, anom,
    op, idx_vm, std_vm, corr_vm, idx_own, idx_in, idx, send, recv, prod, gram, msg1, in1, msg2, in2, l1, r1, l2, r2, gram_in,
    load_sem, idx_sem, idx_send, idx_recv, tile_send, tile_recv, s1, q1, s2, q2, s3, q3,
):
    region, band = lax.axis_index("region"), lax.axis_index("band")
    column, core = region // 2, region % 2
    near = core * BAND + band

    load_anom = pltpu.make_async_copy(anom_hbm, anom, load_sem.at[0])
    load_op = pltpu.make_async_copy(op_hbm, op, load_sem.at[1])
    load_idx = pltpu.make_async_copy(idx_hbm, idx_vm, load_sem.at[2])
    load_std = pltpu.make_async_copy(std_hbm, std_vm, load_sem.at[3])
    load_corr = pltpu.make_async_copy(corr_hbm, corr_vm, load_sem.at[4])
    load_idx.start()

    def near_peer(e):
        p = (core + e // BAND) % 2 * BAND + (band + e % BAND) % BAND
        return (column * 2 + p // BAND, p % BAND), p

    def far_peer(e):
        q = (column // 4 + e // 4) % 4 * 4 + (column % 4 + e % 4) % 4
        return (q * 2 + core, band), q

    barrier = pltpu.get_barrier_semaphore()
    for e in range(1, NEAR):
        pl.semaphore_signal(barrier, inc=1, device_id=near_peer(e)[0], device_id_type=MESH)
    for e in range(1, FAR):
        pl.semaphore_signal(barrier, inc=1, device_id=far_peer(e)[0], device_id_type=MESH)

    load_anom.start()
    load_std.start()
    load_corr.start()
    load_op.start()
    load_idx.wait()
    idx_own[...] = jnp.zeros((8, M), jnp.int32)
    idx_own[0:BAND, 0:BLK] = idx_vm[...]
    own_idx = pltpu.make_async_copy(idx_own, idx.at[0], load_sem.at[2])
    own_idx.start()
    pl.semaphore_wait(barrier, NEAR + FAR - 2)

    def idx_copy(e):
        return pltpu.make_async_remote_copy(
            src_ref=idx_own, dst_ref=idx_in.at[BAND - e], send_sem=idx_send.at[e], recv_sem=idx_recv.at[e],
            device_id=(region, (band + e) % BAND), device_id_type=MESH,
        )

    for e in (1, 3, 2):
        idx_copy(e).start()
    load_anom.wait()

    def tile_copy(k, c):
        part = pl.ds(c * CHUNK, CHUNK)
        return pltpu.make_async_remote_copy(
            src_ref=send.at[k - 1, part], dst_ref=recv.at[k - 1, part],
            send_sem=tile_send.at[k - 1, c], recv_sem=tile_recv.at[k - 1, c],
            device_id=(region, (band + BAND - k) % BAND), device_id_type=MESH,
        )

    def serve(k, c):
        for t in range(CHUNK):
            j = c * CHUNK + t
            send[k - 1, j] = anom[idx[BAND - k, k, j]]
        tile_copy(k, c).start()

    def serve_first(k, c):
        for t in range(CHUNK):
            j = c * CHUNK + t
            send[k - 1, j] = anom[idx_in[BAND - k, k : k + 1, :][0, j]]
        tile_copy(k, c).start()

    def serve_sides(c, carry):
        serve(1, c)
        serve(3, c)
        return carry

    def serve_all(c, carry):
        serve(2, c)
        return serve_sides(c, carry)

    def to_scalar(e):
        return pltpu.make_async_copy(idx_in.at[BAND - e], idx.at[BAND - e], idx_sem.at[e])

    for e in (1, 3):
        idx_copy(e).wait_recv()
        to_scalar(e).start()
        for c in range(LEAD):
            serve_first(e, c)
    for e in (1, 3):
        to_scalar(e).wait()
    idx_copy(2).wait_recv()
    to_scalar(2).start()
    for c in range(LEAD):
        serve_first(2, c)
    to_scalar(2).wait()
    lax.fori_loop(LEAD, CHUNKS, serve_all, 0)
    own_idx.wait()
    load_std.wait()
    load_corr.wait()
    load_op.wait()
    gram[...] = jnp.zeros((M, M), F32)

    def use(c, carry):
        last, product, cross, square = carry
        for k in (1, 3, 2):
            tile_copy(k, c).wait_recv()
        for t in range(CHUNK):
            j = c * CHUNK + t
            value = jnp.dot(op[j, 0], anom[idx[0, 0, j]], preferred_element_type=F32)
            for k in range(1, BAND):
                value = value + jnp.dot(op[j, k], recv[k - 1, j], preferred_element_type=F32)
            value = value * as_columns(1.0 / std_vm[pl.ds(j, 1), :])
            decay, value = block_scan(as_columns(corr_vm[pl.ds(j, 1), :]), value)
            value = value + decay * last
            decay = decay * product
            whit[j] = value
            prod[j] = decay
            last, product = value[M - 1 : M], decay[M - 1 : M]
            gram[...] += jnp.dot(value.T, value, precision=HIGHEST, preferred_element_type=F32)
            cross = cross + jnp.sum(value * decay, axis=0, keepdims=True)
            square = square + jnp.sum(decay * decay, axis=0, keepdims=True)
        return last, product, cross, square

    zero = jnp.zeros((1, M), F32)
    last, product, cross, square = lax.fori_loop(0, CHUNKS, use, (zero, jnp.ones((1, M), F32), zero, zero))

    state = jnp.concatenate([product, last, cross, square], axis=0)
    for p in range(NEAR):
        msg1[p, 0:ROWS] = gram[p * ROWS : (p + 1) * ROWS]
        msg1[p, ROWS : ROWS + 4] = state

    def copy1(e):
        device, p = near_peer(e)
        return pltpu.make_async_remote_copy(
            src_ref=msg1.at[p], dst_ref=in1.at[near], send_sem=s1.at[e], recv_sem=q1.at[e],
            device_id=device, device_id_type=MESH,
        )

    for e in NEAR_ORDER:
        copy1(e).start()
    in1[near] = msg1[near]

    def drain(c, carry):
        for k in range(1, BAND):
            tile_copy(k, c).wait_send()
        return carry

    lax.fori_loop(0, CHUNKS, drain, 0)
    for e in (2, 1, 3):
        idx_copy(e).wait_send()
    for e in range(1, NEAR):
        copy1(e).wait_recv()
    rows, state, own_carry, own_product = combine(NEAR, near, near * ROWS, in1, l1, r1)
    msg2[0:ROWS] = rows
    msg2[ROWS : ROWS + 4] = state

    def copy2(e):
        device, _ = far_peer(e)
        return pltpu.make_async_remote_copy(
            src_ref=msg2, dst_ref=in2.at[column], send_sem=s2.at[e], recv_sem=q2.at[e],
            device_id=device, device_id_type=MESH,
        )

    for e in FAR_ORDER:
        copy2(e).start()
    in2[column] = msg2[...]
    for e in range(1, NEAR):
        copy1(e).wait_send()
    for e in range(1, FAR):
        copy2(e).wait_recv()
    rows, state, far_carry, _ = combine(FAR, column, near * ROWS, in2, l2, r2)
    here = lax.broadcasted_iota(jnp.int32, (ROWS, M), 0) + near * ROWS
    lane = lax.broadcasted_iota(jnp.int32, (ROWS, M), 1)
    rows = rows + jnp.where(here == lane, M - 1.0, 0.0)
    own_rows = pl.ds(pl.multiple_of(near * ROWS, ROWS), ROWS)
    gram_in[own_rows, :] = rows

    def copy3(e):
        device, _ = near_peer(e)
        return pltpu.make_async_remote_copy(
            src_ref=gram_in.at[own_rows], dst_ref=gram_in.at[own_rows], send_sem=s3.at[e], recv_sem=q3.at[e],
            device_id=device, device_id_type=MESH,
        )

    for e in NEAR_ORDER:
        copy3(e).start()

    before = own_carry + own_product * far_carry

    def settle(j, carry):
        whit[j] = whit[j] + prod[j] * before
        return carry

    lax.fori_loop(0, BLK, settle, 0)
    for e in range(1, FAR):
        copy2(e).wait_send()
    for e in range(1, NEAR):
        copy3(e).wait_recv()
    gram_out[...] = gram_in[...]

    for e in range(1, NEAR):
        copy3(e).wait_send()


def inverse_factor(work, gram, spread):
    n = M // 8
    lane = lax.broadcasted_iota(jnp.int32, (8, M), 1)
    sub = lax.broadcasted_iota(jnp.int32, (8, M), 0)
    rows = [gram[8 * i : 8 * i + 8, :] for i in range(n)]
    for p in range(n):
        base = 8 * p
        block = rows[p]
        cols = [jnp.broadcast_to(block[:, base + l : base + l + 1], (8, M)) for l in range(8)]
        side = p % 2 * 64
        for l in range(8):
            spread[side + 8 * l : side + 8 * l + 8, :] = cols[l]
        s = {}
        for l in range(8):
            for j in range(l + 1):
                at = side + 8 * l + j
                s[j, l] = jnp.broadcast_to(spread[at : at + 1, :], (8, M))
        inside = (lane >= base) & (lane < base + 8)
        r = []
        for j in range(8):
            own = jnp.broadcast_to(block[j : j + 1, :], (8, M))
            r.append(jnp.where(inside, jnp.where(lane == base + j, 1.0, 0.0), own))
        lower, pivot = [], []
        for j in range(8):
            inv = 1.0 / s[j, j]
            lower.append(r[j])
            pivot.append(s[j, j])
            for i in range(8):
                if i == j:
                    continue
                f = (s[j, i] if i > j else s[i, j]) * inv
                for l in range(max(i, j + 1), 8):
                    s[i, l] = s[i, l] - f * s[j, l]
                r[i] = r[i] - f * r[j]
            for l in range(j + 1, 8):
                s[j, l] = s[j, l] * inv
            r[j] = r[j] * inv
        out, d = lower[0], pivot[0]
        for j in range(1, 8):
            out = jnp.where(sub == j, lower[j], out)
            d = jnp.where(sub == j, pivot[j], d)
        keep = lane <= base + sub
        work[8 * p : 8 * p + 8, :] = jnp.where(keep, out * lax.rsqrt(d), 0.0)
        for i in range(p + 1, n):
            terms = [jnp.broadcast_to(rows[i][:, base + l : base + l + 1], (8, M)) * r[l] for l in range(8)]
            while len(terms) > 1:
                terms = [a + b for a, b in zip(terms[0::2], terms[1::2])]
            rows[i] = jnp.where(inside, 0.0, rows[i]) - terms[0]


PIECES = 16
PIECE = 128 * M // PIECES


def analyse(gram, whit, anom, whit_out, out_hbm, out, work, spread, out_sem, whit_sem):
    def store(i):
        at = pl.ds(i * PIECE, PIECE)
        return pltpu.make_async_copy(out.at[at], out_hbm.at[at], out_sem.at[i])

    store_whit = pltpu.make_async_copy(whit, whit_out, whit_sem)
    store_whit.start()
    inverse_factor(work, gram[...], spread)
    transform = (math.sqrt(M - 1.0) * work[...].T).astype(BF16)
    for i in range(PIECES):
        at = pl.ds(i * PIECE, PIECE)
        out[at, :] = jnp.dot(anom[at, :], transform, preferred_element_type=F32).astype(BF16)
        store(i).start()
    store_whit.wait()
    for i in range(PIECES):
        store(i).wait()


def local(anomalies, operator, local_tile_index, err_std, err_corr):
    any_spec = pl.BlockSpec(memory_space=pl.ANY)
    vmem = pl.BlockSpec(memory_space=pltpu.VMEM)
    dma = pltpu.SemaphoreType.DMA
    gram, whitened, held = pl.pallas_call(
        observe,
        out_shape=(
            pltpu.VMEM((M, M), F32),
            pltpu.VMEM((BLK, M, M), F32),
            pltpu.VMEM((M, M, M), BF16),
        ),
        in_specs=[any_spec] * 5,
        out_specs=(vmem, vmem, vmem),
        scratch_shapes=[
            pltpu.VMEM((BLK, BAND, M, M), BF16),
            pltpu.VMEM((BAND, BLK), jnp.int32),
            pltpu.VMEM((BLK, M), F32),
            pltpu.VMEM((BLK, M), F32),
            pltpu.VMEM((8, M), jnp.int32),
            pltpu.VMEM((BAND, 8, M), jnp.int32),
            pltpu.SMEM((BAND, 8, M), jnp.int32),
            pltpu.VMEM((BAND - 1, BLK, M, M), BF16),
            pltpu.VMEM((BAND - 1, BLK, M, M), BF16),
            pltpu.VMEM((BLK, M, M), F32),
            pltpu.VMEM((M, M), F32),
            pltpu.VMEM((NEAR, ROWS + 4, M), F32),
            pltpu.VMEM((NEAR, ROWS + 4, M), F32),
            pltpu.VMEM((ROWS + 4, M), F32),
            pltpu.VMEM((FAR, ROWS + 4, M), F32),
            pltpu.VMEM((2 * NEAR, M), F32),
            pltpu.VMEM((2 * NEAR, M), F32),
            pltpu.VMEM((2 * FAR, M), F32),
            pltpu.VMEM((2 * FAR, M), F32),
            pltpu.VMEM((M, M), F32),
            dma((5,)),
            dma((BAND,)),
            dma((BAND,)),
            dma((BAND,)),
            dma((BAND - 1, CHUNKS)),
            dma((BAND - 1, CHUNKS)),
            dma((NEAR,)),
            dma((NEAR,)),
            dma((FAR,)),
            dma((FAR,)),
            dma((NEAR,)),
            dma((NEAR,)),
        ],
        compiler_params=pltpu.CompilerParams(
            collective_id=0, has_side_effects=True, vmem_limit_bytes=OBSERVE_VMEM
        ),
        name="observe",
    )(
        anomalies.reshape(M, M, M),
        operator,
        local_tile_index.T,
        err_std.reshape(BLK, M),
        err_corr.reshape(BLK, M),
    )
    whitened, updated = pl.pallas_call(
        analyse,
        out_shape=(jax.ShapeDtypeStruct((BLK * M, M), F32), jax.ShapeDtypeStruct((M * M, M), BF16)),
        in_specs=[vmem, vmem, vmem],
        out_specs=(any_spec, any_spec),
        scratch_shapes=[
            pltpu.VMEM((M * M, M), BF16),
            pltpu.VMEM((M, M), F32),
            pltpu.VMEM((2 * 64, M), F32),
            dma((PIECES,)),
            dma,
        ],
        compiler_params=pltpu.CompilerParams(vmem_limit_bytes=ANALYSE_VMEM),
        name="analyse",
    )(gram, whitened.reshape(BLK * M, M), held.reshape(M * M, M))
    return whitened, updated


def solution(mesh):
    both = ("region", "band")
    return jax.shard_map(
        local,
        mesh=mesh,
        in_specs=(P(both, None), P(both, None, None, None), P(both, None), P(both), P(both)),
        out_specs=(P(both, None), P(both, None)),
        check_vma=False,
    )
```

```python
import functools
import math

import jax
import jax.numpy as jnp
from jax import lax
from jax.experimental import pallas as pl
from jax.experimental.pallas import tpu as pltpu
from jax.sharding import PartitionSpec as P

MESH = pl.DeviceIdType.MESH
HIGHEST = lax.Precision.HIGHEST
F32 = jnp.float32
BF16 = jnp.bfloat16

M = 128
BLK = 16
BAND = 4
CHUNK = 1
CHUNKS = BLK // CHUNK
LEAD = 2
NEAR = 8
FAR = 16
NEAR_ORDER = (6, 2, 5, 7, 1, 3, 4)
FAR_ORDER = (10, 6, 9, 11, 14, 2, 5, 7, 8, 13, 15, 1, 3, 4, 12)
ROWS = M // NEAR
OBSERVE_VMEM = 52 * 1024 * 1024
ANALYSE_VMEM = 16 * 1024 * 1024


def block_scan(decay, value):
    row = lax.broadcasted_iota(jnp.int32, (M, M), 0)
    for d in (1, 2, 4):
        seen = row >= d
        before_v = jnp.where(seen, pltpu.roll(value, d, 0), 0.0)
        before_d = jnp.where(seen, pltpu.roll(decay, d, 0), 1.0)
        value = value + decay * before_v
        decay = decay * before_d
    for d in (8, 16, 32, 64):
        value = jnp.concatenate([value[:d], value[d:] + decay[d:] * value[:-d]], axis=0)
        decay = jnp.concatenate([decay[:d], decay[d:] * decay[:-d]], axis=0)
    return decay, value


def as_columns(row):
    return jnp.broadcast_to(row, (M, M)).T


def combine(n, me, rows_at, parts, left, right):
    carry = jnp.zeros((1, M), F32)
    product = jnp.ones((1, M), F32)
    cross = jnp.zeros((1, M), F32)
    square = jnp.zeros((1, M), F32)
    own_carry, own_product = carry, product
    rows = jnp.zeros((ROWS, M), F32)
    for i in range(n):
        rows = rows + parts[i, 0:ROWS]
        state = parts[i, ROWS : ROWS + 4]
        a, b, h, s = (state[k : k + 1] for k in range(4))
        mine = me == i
        own_carry = jnp.where(mine, carry, own_carry)
        own_product = jnp.where(mine, product, own_product)
        u = h + s * carry
        left[i : i + 1, :] = h
        left[n + i : n + i + 1, :] = carry
        right[i : i + 1, :] = carry
        right[n + i : n + i + 1, :] = u
        cross = cross + product * u
        square = square + product * product * s
        carry = b + a * carry
        product = product * a
    own = pltpu.roll(left[...], (M - rows_at) % M, 1)[:, 0:ROWS]
    rows = rows + jnp.dot(own.T, right[...], precision=HIGHEST, preferred_element_type=F32)
    state = jnp.concatenate([product, carry, cross, square], axis=0)
    return rows, state, own_carry, own_product


def observe(
    anom_hbm, op_hbm, idx_hbm, std_hbm, corr_hbm,
    gram_out, whit, anom,
    op, idx_vm, std_vm, corr_vm, idx_own, idx_in, idx, send, recv, prod, gram, msg1, in1, msg2, in2, l1, r1, l2, r2, gram_in,
    load_sem, idx_sem, idx_send, idx_recv, tile_send, tile_recv, s1, q1, s2, q2, s3, q3,
):
    region, band = lax.axis_index("region"), lax.axis_index("band")
    column, core = region // 2, region % 2
    near = core * BAND + band

    load_anom = pltpu.make_async_copy(anom_hbm, anom, load_sem.at[0])
    load_op = pltpu.make_async_copy(op_hbm, op, load_sem.at[1])
    load_idx = pltpu.make_async_copy(idx_hbm, idx_vm, load_sem.at[2])
    load_std = pltpu.make_async_copy(std_hbm, std_vm, load_sem.at[3])
    load_corr = pltpu.make_async_copy(corr_hbm, corr_vm, load_sem.at[4])
    load_idx.start()

    def near_peer(e):
        p = (core + e // BAND) % 2 * BAND + (band + e % BAND) % BAND
        return (column * 2 + p // BAND, p % BAND), p

    def far_peer(e):
        q = (column // 4 + e // 4) % 4 * 4 + (column % 4 + e % 4) % 4
        return (q * 2 + core, band), q

    barrier = pltpu.get_barrier_semaphore()
    for e in range(1, NEAR):
        pl.semaphore_signal(barrier, inc=1, device_id=near_peer(e)[0], device_id_type=MESH)
    for e in range(1, FAR):
        pl.semaphore_signal(barrier, inc=1, device_id=far_peer(e)[0], device_id_type=MESH)

    load_anom.start()
    load_std.start()
    load_corr.start()
    load_op.start()
    load_idx.wait()
    idx_own[...] = jnp.zeros((8, M), jnp.int32)
    idx_own[0:BAND, 0:BLK] = idx_vm[...]
    own_idx = pltpu.make_async_copy(idx_own, idx.at[0], load_sem.at[2])
    own_idx.start()
    pl.semaphore_wait(barrier, NEAR + FAR - 2)

    def idx_copy(e):
        return pltpu.make_async_remote_copy(
            src_ref=idx_own, dst_ref=idx_in.at[BAND - e], send_sem=idx_send.at[e], recv_sem=idx_recv.at[e],
            device_id=(region, (band + e) % BAND), device_id_type=MESH,
        )

    for e in (1, 3, 2):
        idx_copy(e).start()
    load_anom.wait()

    def tile_copy(k, c):
        part = pl.ds(c * CHUNK, CHUNK)
        return pltpu.make_async_remote_copy(
            src_ref=send.at[k - 1, part], dst_ref=recv.at[k - 1, part],
            send_sem=tile_send.at[k - 1, c], recv_sem=tile_recv.at[k - 1, c],
            device_id=(region, (band + BAND - k) % BAND), device_id_type=MESH,
        )

    def serve(k, c):
        for t in range(CHUNK):
            j = c * CHUNK + t
            send[k - 1, j] = anom[idx[BAND - k, k, j]]
        tile_copy(k, c).start()

    def serve_first(k, c):
        for t in range(CHUNK):
            j = c * CHUNK + t
            send[k - 1, j] = anom[idx_in[BAND - k, k : k + 1, :][0, j]]
        tile_copy(k, c).start()

    def serve_sides(c, carry):
        serve(1, c)
        serve(3, c)
        return carry

    def serve_all(c, carry):
        serve(2, c)
        return serve_sides(c, carry)

    def to_scalar(e):
        return pltpu.make_async_copy(idx_in.at[BAND - e], idx.at[BAND - e], idx_sem.at[e])

    for e in (1, 3):
        idx_copy(e).wait_recv()
        to_scalar(e).start()
    for c in range(LEAD):
        for k in (1, 3):
            serve_first(k, c)
    for e in (1, 3):
        to_scalar(e).wait()
    idx_copy(2).wait_recv()
    to_scalar(2).start()
    for c in range(LEAD):
        serve_first(2, c)
    to_scalar(2).wait()
    lax.fori_loop(LEAD, CHUNKS, serve_all, 0)
    own_idx.wait()
    load_std.wait()
    load_corr.wait()
    load_op.wait()
    gram[...] = jnp.zeros((M, M), F32)

    def use(c, carry):
        last, product, cross, square = carry
        for k in (1, 3, 2):
            tile_copy(k, c).wait_recv()
        for t in range(CHUNK):
            j = c * CHUNK + t
            value = jnp.dot(op[j, 0], anom[idx[0, 0, j]], preferred_element_type=F32)
            for k in range(1, BAND):
                value = value + jnp.dot(op[j, k], recv[k - 1, j], preferred_element_type=F32)
            value = value * as_columns(1.0 / std_vm[pl.ds(j, 1), :])
            decay, value = block_scan(as_columns(corr_vm[pl.ds(j, 1), :]), value)
            value = value + decay * last
            decay = decay * product
            whit[j] = value
            prod[j] = decay
            last, product = value[M - 1 : M], decay[M - 1 : M]
            gram[...] += jnp.dot(value.T, value, precision=HIGHEST, preferred_element_type=F32)
            cross = cross + jnp.sum(value * decay, axis=0, keepdims=True)
            square = square + jnp.sum(decay * decay, axis=0, keepdims=True)
        return last, product, cross, square

    zero = jnp.zeros((1, M), F32)
    last, product, cross, square = lax.fori_loop(0, CHUNKS, use, (zero, jnp.ones((1, M), F32), zero, zero))

    state = jnp.concatenate([product, last, cross, square], axis=0)
    for p in range(NEAR):
        msg1[p, 0:ROWS] = gram[p * ROWS : (p + 1) * ROWS]
        msg1[p, ROWS : ROWS + 4] = state

    def copy1(e):
        device, p = near_peer(e)
        return pltpu.make_async_remote_copy(
            src_ref=msg1.at[p], dst_ref=in1.at[near], send_sem=s1.at[e], recv_sem=q1.at[e],
            device_id=device, device_id_type=MESH,
        )

    for e in NEAR_ORDER:
        copy1(e).start()
    in1[near] = msg1[near]

    def drain(c, carry):
        for k in range(1, BAND):
            tile_copy(k, c).wait_send()
        return carry

    lax.fori_loop(0, CHUNKS, drain, 0)
    for e in (2, 1, 3):
        idx_copy(e).wait_send()
    for e in range(1, NEAR):
        copy1(e).wait_recv()
    rows, state, own_carry, own_product = combine(NEAR, near, near * ROWS, in1, l1, r1)
    msg2[0:ROWS] = rows
    msg2[ROWS : ROWS + 4] = state

    def copy2(e):
        device, _ = far_peer(e)
        return pltpu.make_async_remote_copy(
            src_ref=msg2, dst_ref=in2.at[column], send_sem=s2.at[e], recv_sem=q2.at[e],
            device_id=device, device_id_type=MESH,
        )

    for e in FAR_ORDER:
        copy2(e).start()
    in2[column] = msg2[...]
    for e in range(1, NEAR):
        copy1(e).wait_send()
    for e in range(1, FAR):
        copy2(e).wait_recv()
    rows, state, far_carry, _ = combine(FAR, column, near * ROWS, in2, l2, r2)
    here = lax.broadcasted_iota(jnp.int32, (ROWS, M), 0) + near * ROWS
    lane = lax.broadcasted_iota(jnp.int32, (ROWS, M), 1)
    rows = rows + jnp.where(here == lane, M - 1.0, 0.0)
    own_rows = pl.ds(pl.multiple_of(near * ROWS, ROWS), ROWS)
    gram_in[own_rows, :] = rows

    def copy3(e):
        device, _ = near_peer(e)
        return pltpu.make_async_remote_copy(
            src_ref=gram_in.at[own_rows], dst_ref=gram_in.at[own_rows], send_sem=s3.at[e], recv_sem=q3.at[e],
            device_id=device, device_id_type=MESH,
        )

    for e in NEAR_ORDER:
        copy3(e).start()

    before = own_carry + own_product * far_carry

    def settle(j, carry):
        whit[j] = whit[j] + prod[j] * before
        return carry

    lax.fori_loop(0, BLK, settle, 0)
    for e in range(1, FAR):
        copy2(e).wait_send()
    for e in range(1, NEAR):
        copy3(e).wait_recv()
    gram_out[...] = gram_in[...]

    for e in range(1, NEAR):
        copy3(e).wait_send()


def inverse_factor(work, gram, spread):
    n = M // 8
    lane = lax.broadcasted_iota(jnp.int32, (8, M), 1)
    sub = lax.broadcasted_iota(jnp.int32, (8, M), 0)
    rows = [gram[8 * i : 8 * i + 8, :] for i in range(n)]
    for p in range(n):
        base = 8 * p
        block = rows[p]
        cols = [jnp.broadcast_to(block[:, base + l : base + l + 1], (8, M)) for l in range(8)]
        side = p % 2 * 64
        for l in range(8):
            spread[side + 8 * l : side + 8 * l + 8, :] = cols[l]
        s = {}
        for l in range(8):
            for j in range(l + 1):
                at = side + 8 * l + j
                s[j, l] = jnp.broadcast_to(spread[at : at + 1, :], (8, M))
        inside = (lane >= base) & (lane < base + 8)
        r = []
        for j in range(8):
            own = jnp.broadcast_to(block[j : j + 1, :], (8, M))
            r.append(jnp.where(inside, jnp.where(lane == base + j, 1.0, 0.0), own))
        lower, pivot = [], []
        for j in range(8):
            inv = 1.0 / s[j, j]
            lower.append(r[j])
            pivot.append(s[j, j])
            for i in range(8):
                if i == j:
                    continue
                f = (s[j, i] if i > j else s[i, j]) * inv
                for l in range(max(i, j + 1), 8):
                    s[i, l] = s[i, l] - f * s[j, l]
                r[i] = r[i] - f * r[j]
            for l in range(j + 1, 8):
                s[j, l] = s[j, l] * inv
            r[j] = r[j] * inv
        out, d = lower[0], pivot[0]
        for j in range(1, 8):
            out = jnp.where(sub == j, lower[j], out)
            d = jnp.where(sub == j, pivot[j], d)
        keep = lane <= base + sub
        work[8 * p : 8 * p + 8, :] = jnp.where(keep, out * lax.rsqrt(d), 0.0)
        for i in range(p + 1, n):
            terms = [jnp.broadcast_to(rows[i][:, base + l : base + l + 1], (8, M)) * r[l] for l in range(8)]
            while len(terms) > 1:
                terms = [a + b for a, b in zip(terms[0::2], terms[1::2])]
            rows[i] = jnp.where(inside, 0.0, rows[i]) - terms[0]


PIECES = 16
PIECE = 128 * M // PIECES


def analyse(gram, whit, anom, whit_out, out_hbm, out, work, spread, out_sem, whit_sem):
    def store(i):
        at = pl.ds(i * PIECE, PIECE)
        return pltpu.make_async_copy(out.at[at], out_hbm.at[at], out_sem.at[i])

    store_whit = pltpu.make_async_copy(whit, whit_out, whit_sem)
    inverse_factor(work, gram[...], spread)
    store_whit.start()
    transform = (math.sqrt(M - 1.0) * work[...].T).astype(BF16)
    for i in range(PIECES):
        at = pl.ds(i * PIECE, PIECE)
        out[at, :] = jnp.dot(anom[at, :], transform, preferred_element_type=F32).astype(BF16)
        store(i).start()
    store_whit.wait()
    for i in range(PIECES):
        store(i).wait()


def local(anomalies, operator, local_tile_index, err_std, err_corr):
    any_spec = pl.BlockSpec(memory_space=pl.ANY)
    vmem = pl.BlockSpec(memory_space=pltpu.VMEM)
    dma = pltpu.SemaphoreType.DMA
    gram, whitened, held = pl.pallas_call(
        observe,
        out_shape=(
            pltpu.VMEM((M, M), F32),
            pltpu.VMEM((BLK, M, M), F32),
            pltpu.VMEM((M, M, M), BF16),
        ),
        in_specs=[any_spec] * 5,
        out_specs=(vmem, vmem, vmem),
        scratch_shapes=[
            pltpu.VMEM((BLK, BAND, M, M), BF16),
            pltpu.VMEM((BAND, BLK), jnp.int32),
            pltpu.VMEM((BLK, M), F32),
            pltpu.VMEM((BLK, M), F32),
            pltpu.VMEM((8, M), jnp.int32),
            pltpu.VMEM((BAND, 8, M), jnp.int32),
            pltpu.SMEM((BAND, 8, M), jnp.int32),
            pltpu.VMEM((BAND - 1, BLK, M, M), BF16),
            pltpu.VMEM((BAND - 1, BLK, M, M), BF16),
            pltpu.VMEM((BLK, M, M), F32),
            pltpu.VMEM((M, M), F32),
            pltpu.VMEM((NEAR, ROWS + 4, M), F32),
            pltpu.VMEM((NEAR, ROWS + 4, M), F32),
            pltpu.VMEM((ROWS + 4, M), F32),
            pltpu.VMEM((FAR, ROWS + 4, M), F32),
            pltpu.VMEM((2 * NEAR, M), F32),
            pltpu.VMEM((2 * NEAR, M), F32),
            pltpu.VMEM((2 * FAR, M), F32),
            pltpu.VMEM((2 * FAR, M), F32),
            pltpu.VMEM((M, M), F32),
            dma((5,)),
            dma((BAND,)),
            dma((BAND,)),
            dma((BAND,)),
            dma((BAND - 1, CHUNKS)),
            dma((BAND - 1, CHUNKS)),
            dma((NEAR,)),
            dma((NEAR,)),
            dma((FAR,)),
            dma((FAR,)),
            dma((NEAR,)),
            dma((NEAR,)),
        ],
        compiler_params=pltpu.CompilerParams(
            collective_id=0, has_side_effects=True, vmem_limit_bytes=OBSERVE_VMEM
        ),
        name="observe",
    )(
        anomalies.reshape(M, M, M),
        operator,
        local_tile_index.T,
        err_std.reshape(BLK, M),
        err_corr.reshape(BLK, M),
    )
    whitened, updated = pl.pallas_call(
        analyse,
        out_shape=(jax.ShapeDtypeStruct((BLK * M, M), F32), jax.ShapeDtypeStruct((M * M, M), BF16)),
        in_specs=[vmem, vmem, vmem],
        out_specs=(any_spec, any_spec),
        scratch_shapes=[
            pltpu.VMEM((M * M, M), BF16),
            pltpu.VMEM((M, M), F32),
            pltpu.VMEM((2 * 64, M), F32),
            dma((PIECES,)),
            dma,
        ],
        compiler_params=pltpu.CompilerParams(vmem_limit_bytes=ANALYSE_VMEM),
        name="analyse",
    )(gram, whitened.reshape(BLK * M, M), held.reshape(M * M, M))
    return whitened, updated


def solution(mesh):
    both = ("region", "band")
    return jax.shard_map(
        local,
        mesh=mesh,
        in_specs=(P(both, None), P(both, None, None, None), P(both, None), P(both), P(both)),
        out_specs=(P(both, None), P(both, None)),
        check_vma=False,
    )
```
